128 devices in a mesh: depth: 2 (over core), row: 16 (over x, z), col: 4 (over y).
Axes of the slice: x: 4, y: 4, z: 4, core: 2. Of those that a mesh axis runs over, the one named last changes fastest.
Arguments:
- layer_input: bfloat16 [1024, 8192], P(('depth', 'row'), 'col'), may hold values from -6 to 6
- w_in: bfloat16 [8192, 24576], P('col', 'row'), may hold values from -0.0625 to 0.0625
- w_out: bfloat16 [24576, 8192], P('row', 'col'), may hold values from -0.0390625 to 0.0390625
- output_grad: bfloat16 [1024, 8192], P(('depth', 'row'), 'col'), may hold values from -1.5 to 1.5
Outputs:
- block_output: bfloat16 [1024, 8192], P(('depth', 'row'), 'col')
- input_grad: bfloat16 [1024, 8192], P(('depth', 'row'), 'col')
- w_in_grad: bfloat16 [8192, 24576], P('col', 'row')
- w_out_grad: bfloat16 [24576, 8192], P('row', 'col')
The draws below stay inside these ranges and needn't reach their ends.
All inputs are finite; a program needn't handle non-finite values.
Results may differ from the reference program's by a relative error of at most 0.0059.
Values may be sent and summed in bfloat16 or wider, within the bound.
A program may use at most 192 MiB of HBM per device.

```python
import math
import jax
import jax.numpy as jnp
from jax import lax

D = 8192
FF = 24576
TOKENS = 1024
N_DEPTH = 2


def steps_of(stream_key, dims, split, least, top_value):
    level = 1.0
    for axis_at, shards_of in split:
        heights = jax.random.uniform(jax.random.fold_in(jax.random.fold_in(stream_key, 6), axis_at), (shards_of,), jnp.float32, least / len(split), top_value / len(split))
        level = level * jnp.repeat(jnp.exp(heights), dims[axis_at] // shards_of).reshape((-1,) + (1,) * (len(dims) - 1 - axis_at))
    return level


def centred(rng, extent, width, most, shards=(), held_as=jnp.bfloat16):
    entries = jax.random.normal(rng, extent, jnp.float32) * width
    if len(shards) > 0:
        entries = steps_of(rng, extent, shards, -0.22, 0.18) * entries
    return jnp.clip(entries, min=-most, max=most).astype(held_as)


def setup_inputs(seed: int = 0) -> dict:
    keys = jax.random.split(jax.random.key(seed), 5)
    return {
        "layer_input": centred(keys[0], (TOKENS, D), 1.0, 6.0, ((0, 32), (1, 4))),
        "w_in": centred(keys[1], (D, FF), D ** -0.5, 0.0625, ((0, 4), (1, 16))),
        "w_out": centred(keys[2], (FF, D), FF ** -0.5, 0.0390625, ((0, 16), (1, 4))),
        "output_grad": centred(keys[3], (TOKENS, D), 0.25, 1.5, ((0, 32), (1, 4))),
    }


def gelu_parts(hidden):
    coeff = math.sqrt(2.0 / math.pi)
    cubic = hidden * hidden * hidden
    tangent = jnp.tanh(coeff * (hidden + 0.044715 * cubic))
    value = 0.5 * hidden * (1.0 + tangent)
    slope = 0.5 * (1.0 + tangent) + 0.5 * hidden * (1.0 - tangent * tangent) * coeff * (1.0 + 3.0 * 0.044715 * hidden * hidden)
    return (value, slope)

def reference(layer_input, w_in, w_out, output_grad):
    hidden = jnp.dot(layer_input, w_in, preferred_element_type=jnp.float32)
    value, slope = gelu_parts(hidden)
    activ = value.astype(jnp.bfloat16)
    mixed = jnp.dot(activ, w_out, preferred_element_type=jnp.float32)
    block_output = (layer_input.astype(jnp.float32) + mixed).astype(jnp.bfloat16)
    grad_act = lax.dot_general(output_grad, w_out, (((1,), (1,)), ((), ())), preferred_element_type=jnp.float32)
    grad_hid = (grad_act * slope).astype(jnp.bfloat16)
    back = lax.dot_general(grad_hid, w_in, (((1,), (1,)), ((), ())), preferred_element_type=jnp.float32)
    input_grad = (output_grad.astype(jnp.float32) + back).astype(jnp.bfloat16)
    layer_len = layer_input.shape[0] // N_DEPTH
    total_in = jnp.zeros((w_in.shape[0], w_in.shape[1]), jnp.float32)
    total_out = jnp.zeros((w_out.shape[0], w_out.shape[1]), jnp.float32)
    for layer in range(N_DEPTH):
        lo = layer * layer_len
        part_in = lax.dot_general(layer_input[lo:lo + layer_len], grad_hid[lo:lo + layer_len], (((0,), (0,)), ((), ())), preferred_element_type=jnp.float32)
        part_in = lax.optimization_barrier(part_in.astype(jnp.bfloat16))
        total_in = total_in + part_in.astype(jnp.float32)
        part_out = lax.dot_general(activ[lo:lo + layer_len], output_grad[lo:lo + layer_len], (((0,), (0,)), ((), ())), preferred_element_type=jnp.float32)
        part_out = lax.optimization_barrier(part_out.astype(jnp.bfloat16))
        total_out = total_out + part_out.astype(jnp.float32)
    return (block_output, input_grad, total_in.astype(jnp.bfloat16), total_out.astype(jnp.bfloat16))
```

```python
import math

import jax
import jax.numpy as jnp
from jax import lax
from jax.experimental import pallas as pl
from jax.experimental.pallas import tpu as pltpu
from jax.sharding import PartitionSpec as P

MESH = pl.DeviceIdType.MESH
SIDE = 4
OWN, PREV, NEXT, FAR = range(4)
CHUNKS = (
    ((OWN, 0, 4),),
    ((PREV, 0, 2), (NEXT, 0, 2)),
    ((PREV, 2, 4), (NEXT, 2, 4)),
    ((FAR, 0, 4),),
)
LO, HI = pl.ds(0, 2), pl.ds(2, 2)
TOP, END = pl.ds(0, 16), pl.ds(16, 16)
N_SEMS = 420


def gelu_parts(hidden):
    coeff = math.sqrt(2.0 / math.pi)
    square = hidden * hidden
    tangent = jnp.tanh(coeff * (hidden + 0.044715 * (square * hidden)))
    value = 0.5 * hidden * (1.0 + tangent)
    slope = 0.5 * (1.0 + tangent) + 0.5 * hidden * (1.0 - tangent * tangent) * coeff * (
        1.0 + 3.0 * 0.044715 * square
    )
    return (value, slope)


def f32(value):
    return value.astype(jnp.float32)


def b16(value):
    return value.astype(jnp.bfloat16)


class Ring:
    def __init__(self, after, before):
        self.after = after
        self.before = before


def block_kernel(
    x_ref, dy_ref, w_in_hbm, w_out_hbm,
    out_ref, grad_ref, x_hbm, dy_hbm, g_hbm, dh_hbm,
    w_in, w_out, x_all, dy_all, g_all, dh_all, slope,
    ysum, yfwd, yback, zsum, zfwd, zback, zown, xsum, xfwd, xback,
    sems,
):
    layer = lax.axis_index("depth")
    row = lax.axis_index("row")
    col = lax.axis_index("col")
    across, along = row // SIDE, row % SIDE

    def device(d, i, k, c):
        return (d, ((i + SIDE) % SIDE) * SIDE + (k + SIDE) % SIDE, (c + SIDE) % SIDE)

    ring_x = Ring(device(layer, across + 1, along, col), device(layer, across - 1, along, col))
    ring_z = Ring(device(layer, across, along + 1, col), device(layer, across, along - 1, col))
    ring_y = Ring(device(layer, across, along, col + 1), device(layer, across, along, col - 1))
    twin = (1 - layer, row, col)

    count = [0]
    sent = []

    def sem():
        count[0] += 1
        return sems.at[count[0] - 1]

    def send(src, dst, to):
        copy = pltpu.make_async_remote_copy(
            src_ref=src, dst_ref=dst, send_sem=sem(), recv_sem=sem(),
            device_id=to, device_id_type=MESH,
        )
        copy.start()
        sent.append(copy.wait_send)
        return copy

    def local(src, dst):
        copy = pltpu.make_async_copy(src, dst, sem())
        copy.start()
        return copy

    load_in = local(w_in_hbm, w_in)
    load_out = local(w_out_hbm, w_out)

    barrier = pltpu.get_barrier_semaphore()
    greeted = (ring_x.after, ring_x.before, ring_z.after, ring_z.before)
    greeted += (ring_y.after, ring_y.before, twin)
    for other in greeted:
        pl.semaphore_signal(barrier, inc=1, device_id=other, device_id_type=MESH)
    x_all[OWN, OWN] = x_ref[...]
    dy_all[OWN, OWN] = dy_ref[...]
    pl.semaphore_wait(barrier, len(greeted))

    def first_sends(every, ring):
        own = every.at[OWN, OWN]
        return (
            send(own, every.at[OWN, PREV], ring.after),
            send(own, every.at[OWN, NEXT], ring.before),
        )

    def plane_send(every, ring, block):
        own = every.at[OWN, block]
        return (
            send(own, every.at[PREV, block], ring.after),
            send(own, every.at[NEXT, block], ring.before),
        )

    stage1_x = first_sends(x_all, ring_x)
    stage1_dy = first_sends(dy_all, ring_z)
    planes_x = [plane_send(x_all, ring_z, OWN)]
    planes_dy = [plane_send(dy_all, ring_x, OWN)]
    far_x, far_dy = [], []
    for every, stage1, planes, far, first, second in (
        (x_all, stage1_x, planes_x, far_x, ring_x, ring_z),
        (dy_all, stage1_dy, planes_dy, far_dy, ring_z, ring_x),
    ):
        stage1[0].wait_recv()
        far.append(send(every.at[OWN, PREV, TOP], every.at[OWN, FAR, TOP], first.after))
        planes.append(plane_send(every, second, PREV))
        stage1[1].wait_recv()
        far.append(send(every.at[OWN, NEXT, END], every.at[OWN, FAR, END], first.before))
        planes.append(plane_send(every, second, NEXT))
    for every, planes, far, second in (
        (x_all, planes_x, far_x, ring_z),
        (dy_all, planes_dy, far_dy, ring_x),
    ):
        far[0].wait_recv()
        far[1].wait_recv()
        planes.append(plane_send(every, second, FAR))

    width = slope.shape[-1]

    def rows_of(every, chunk):
        parts = [every[plane, pl.ds(lo, hi - lo)] for plane, lo, hi in CHUNKS[chunk]]
        part = parts[0] if len(parts) == 1 else jnp.concatenate(parts, axis=0)
        return part.reshape(part.shape[0] * part.shape[1], part.shape[2])

    def y_product(kind, chunk):
        mine = ysum.at[kind, chunk]
        every = (x_all, dy_all)[kind]

        @pl.loop(0, 2)
        def _(tile):
            span = pl.ds(pl.multiple_of(tile * 2 * width, 2 * width), 2 * width)
            lhs = rows_of(every, chunk)
            if kind == 0:
                part = jnp.dot(lhs, w_in[:, span], preferred_element_type=jnp.float32)
            else:
                part = lax.dot_general(
                    lhs, w_out[span, :], (((1,), (1,)), ((), ())),
                    preferred_element_type=jnp.float32,
                )
            part = b16(part)
            for half in range(2):
                shard = (2 * tile + half + SIDE - col) % SIDE
                cut = part[:, half * width : (half + 1) * width]
                mine[shard] = cut.reshape(4, cut.shape[0] // 4, width)

        fwd, back = yfwd.at[kind, chunk], yback.at[kind, chunk]
        return [
            send(mine.at[2, HI], fwd.at[0], ring_y.after),
            send(mine.at[2, LO], fwd.at[1], ring_y.before),
            send(mine.at[1, LO], back.at[0, LO], ring_y.after),
            send(mine.at[3, HI], back.at[1, HI], ring_y.before),
        ]

    def y_relay(kind, chunk, copies):
        mine, fwd, back = ysum.at[kind, chunk], yfwd.at[kind, chunk], yback.at[kind, chunk]
        copies[0].wait_recv()
        mine[1, HI] = b16(f32(mine[1, HI]) + f32(fwd[0]))
        copies.append(send(mine.at[1, HI], back.at[0, HI], ring_y.after))
        copies[1].wait_recv()
        mine[3, LO] = b16(f32(mine[3, LO]) + f32(fwd[1]))
        copies.append(send(mine.at[3, LO], back.at[1, LO], ring_y.before))

    def y_total(kind, chunk, copies):
        for copy in copies[2:]:
            copy.wait_recv()
        mine, back = ysum.at[kind, chunk], yback.at[kind, chunk]
        return f32(mine[0]) + f32(back[0]) + f32(back[1])

    own_columns = pl.ds(pl.multiple_of(col * width, width), width)

    def finish_hidden(chunk, copies):
        value, steep = gelu_parts(y_total(0, chunk, copies))
        value = b16(value)
        at = 0
        for plane, lo, hi in CHUNKS[chunk]:
            g_all[plane, pl.ds(lo, hi - lo), :, own_columns] = value[at : at + hi - lo]
            slope[plane, pl.ds(lo, hi - lo)] = steep[at : at + hi - lo]
            at += hi - lo

    def finish_grad(chunk, copies):
        total = y_total(1, chunk, copies)
        at = 0
        for plane, lo, hi in CHUNKS[chunk]:
            for block in range(lo, hi):
                dh_all[plane, block, :, own_columns] = b16(total[at] * slope[block, plane])
                at += 1

    def gather_wait(planes, block):
        for copy in planes[block]:
            copy.wait_recv()

    c = {}
    load_in.wait()
    c["h0"] = y_product(0, 0)
    load_out.wait()
    c["a0"] = y_product(1, 0)
    fars = {}
    for every, planes, second, name in (
        (x_all, planes_x, ring_z, "x"), (dy_all, planes_dy, ring_x, "dy"),
    ):
        gather_wait(planes, OWN)
        gather_wait(planes, PREV)
        fars[name] = [send(every.at[PREV, LO], every.at[FAR, LO], second.after)]
    c["h1"] = y_product(0, 1)
    y_relay(0, 0, c["h0"])
    c["a1"] = y_product(1, 1)
    y_relay(1, 0, c["a0"])
    for every, planes, second, name in (
        (x_all, planes_x, ring_z, "x"), (dy_all, planes_dy, ring_x, "dy"),
    ):
        gather_wait(planes, NEXT)
        gather_wait(planes, FAR)
        fars[name].append(send(every.at[NEXT, HI], every.at[FAR, HI], second.before))
    c["h2"] = y_product(0, 2)
    y_relay(0, 1, c["h1"])
    c["a2"] = y_product(1, 2)
    y_relay(1, 1, c["a1"])
    finish_hidden(0, c["h0"])
    for copy in fars["x"]:
        copy.wait_recv()
    c["h3"] = y_product(0, 3)
    y_relay(0, 2, c["h2"])
    for copy in fars["dy"]:
        copy.wait_recv()
    c["a3"] = y_product(1, 3)

    keep = []
    shared = []
    for plane in range(4):
        keep.append(local(x_all.at[plane], x_hbm.at[layer, plane]))
        shared.append(send(x_all.at[plane], x_hbm.at[layer, plane], twin))
        keep.append(local(dy_all.at[plane], dy_hbm.at[layer, :, plane]))
        shared.append(send(dy_all.at[plane], dy_hbm.at[layer, :, plane], twin))

    y_relay(1, 2, c["a2"])
    finish_hidden(1, c["h1"])
    finish_hidden(2, c["h2"])

    def y_gather(every, plane):
        own = every.at[plane, :, :, own_columns]
        return [send(own, own, ring_y.after), send(own, own, ring_y.before)]

    def columns_of(step):
        at = (col + step + SIDE) % SIDE
        return pl.ds(pl.multiple_of(at * width, width), width)

    def y_pass(every, plane, copies):
        copies[0].wait_recv()
        part = every.at[plane, LO, :, columns_of(-1)]
        copies.append(send(part, part, ring_y.after))
        copies[1].wait_recv()
        part = every.at[plane, HI, :, columns_of(1)]
        copies.append(send(part, part, ring_y.before))

    def product(kind, plane):
        every = (g_all, dh_all)[kind]

        @pl.loop(0, 4)
        def _(tile):
            cols = w_out.shape[1] // 4
            span = pl.ds(pl.multiple_of(tile * cols, cols), cols)
            lhs = every[plane].reshape(-1, every.shape[-1])
            if kind == 0:
                part = jnp.dot(lhs, w_out[:, span], preferred_element_type=jnp.float32)
            else:
                part = lax.dot_general(
                    lhs, w_in[span, :], (((1,), (1,)), ((), ())),
                    preferred_element_type=jnp.float32,
                )
            part = part.reshape(4, part.shape[0] // 4, cols)
            if plane == OWN:
                zown[kind, :, :, span] = part
            else:
                zsum[kind, plane, :, :, span] = b16(part)

    def planes_start(kind, plane, ring):
        mine, fwd, back = zsum.at[kind], zfwd.at[kind], zback.at[kind]
        if plane == FAR:
            return [
                send(mine.at[FAR, HI], fwd.at[0], ring.after),
                send(mine.at[FAR, LO], fwd.at[1], ring.before),
            ]
        if plane == NEXT:
            return [send(mine.at[NEXT, LO], back.at[0, LO], ring.after)]
        return [send(mine.at[PREV, HI], back.at[1, HI], ring.before)]

    def planes_relay(kind, copies, ring):
        mine, fwd, back = zsum.at[kind], zfwd.at[kind], zback.at[kind]
        copies[FAR][0].wait_recv()
        mine[NEXT, HI] = b16(f32(mine[NEXT, HI]) + f32(fwd[0]))
        copies[NEXT].append(send(mine.at[NEXT, HI], back.at[0, HI], ring.after))
        copies[FAR][1].wait_recv()
        mine[PREV, LO] = b16(f32(mine[PREV, LO]) + f32(fwd[1]))
        copies[PREV].append(send(mine.at[PREV, LO], back.at[1, LO], ring.before))

    def blocks_start(kind, copies, ring):
        for copy in copies[NEXT] + copies[PREV]:
            copy.wait_recv()
        for block in (FAR, NEXT, PREV, OWN):
            total = zown[kind, block] + f32(zback[kind, 0, block]) + f32(zback[kind, 1, block])
            if block == OWN:
                zown[kind, OWN] = total
            else:
                xsum[kind, block] = b16(total)
        mine, fwd, back = xsum.at[kind], xfwd.at[kind], xback.at[kind]
        return [
            send(mine.at[FAR, END], fwd.at[0], ring.after),
            send(mine.at[FAR, TOP], fwd.at[1], ring.before),
            send(mine.at[NEXT, TOP], back.at[0, TOP], ring.after),
            send(mine.at[PREV, END], back.at[1, END], ring.before),
        ]

    def blocks_relay(kind, copies, ring):
        mine, fwd, back = xsum.at[kind], xfwd.at[kind], xback.at[kind]
        copies[0].wait_recv()
        mine[NEXT, END] = b16(f32(mine[NEXT, END]) + f32(fwd[0]))
        copies.append(send(mine.at[NEXT, END], back.at[0, END], ring.after))
        copies[1].wait_recv()
        mine[PREV, TOP] = b16(f32(mine[PREV, TOP]) + f32(fwd[1]))
        copies.append(send(mine.at[PREV, TOP], back.at[1, TOP], ring.before))

    def blocks_total(kind, copies):
        for copy in copies[2:]:
            copy.wait_recv()
        return zown[kind, OWN] + f32(xback[kind, 0]) + f32(xback[kind, 1])

    passes = {}
    moves = {0: {}, 1: {}}
    rings = (ring_z, ring_x)

    def start(name):
        kind, plane = name
        passes[name] = y_gather((g_all, dh_all)[kind], plane)

    def relay(name):
        kind, plane = name
        y_pass((g_all, dh_all)[kind], plane, passes[name])

    def finish(name):
        kind, plane = name
        for copy in passes[name][2:]:
            copy.wait_recv()
        every, kept = ((g_all, g_hbm), (dh_all, dh_hbm))[kind]
        to = kept.at[layer, plane] if kind == 0 else kept.at[layer, :, plane]
        keep.append(local(every.at[plane], to))
        shared.append(send(every.at[plane], to, twin))
        product(kind, plane)
        if plane != OWN:
            moves[kind][plane] = planes_start(kind, plane, rings[kind])

    start((0, PREV))
    y_relay(0, 3, c["h3"])
    start((0, NEXT))
    y_relay(1, 3, c["a3"])
    finish_hidden(3, c["h3"])
    relay((0, PREV))
    start((0, FAR))
    for chunk in range(4):
        finish_grad(chunk, c["a" + str(chunk)])
    relay((0, NEXT))
    start((1, FAR))
    finish((0, PREV))
    relay((0, FAR))
    start((1, NEXT))
    finish((0, NEXT))
    relay((1, FAR))
    start((1, PREV))
    finish((0, FAR))
    relay((1, NEXT))
    start((0, OWN))
    finish((1, FAR))
    planes_relay(0, moves[0], ring_z)
    relay((1, PREV))
    start((1, OWN))
    finish((1, NEXT))
    relay((0, OWN))
    finish((1, PREV))
    relay((1, OWN))
    planes_relay(1, moves[1], ring_x)
    finish((0, OWN))
    last_out = blocks_start(0, moves[0], ring_x)
    finish((1, OWN))
    last_grad = blocks_start(1, moves[1], ring_z)
    blocks_relay(0, last_out, ring_x)
    blocks_relay(1, last_grad, ring_z)
    out_ref[...] = f32(x_ref[...]) + blocks_total(0, last_out)
    grad_ref[...] = f32(dy_ref[...]) + blocks_total(1, last_grad)

    for copy in keep:
        copy.wait()
    for copy in shared:
        copy.wait_recv()
    for wait_send in sent:
        wait_send()


def run_block(x, dy, w_in, w_out):
    tokens, features = x.shape
    hidden = w_in.shape[1]
    width = hidden // SIDE
    every = (4, 4, tokens, features)
    bf, fl = jnp.bfloat16, jnp.float32
    vmem = pl.BlockSpec(memory_space=pltpu.VMEM)
    hbm = pl.BlockSpec(memory_space=pl.ANY)
    shape = jax.ShapeDtypeStruct
    return pl.pallas_call(
        block_kernel,
        out_shape=(
            shape((tokens, features), fl),
            shape((tokens, features), fl),
            shape((2,) + every, bf),
            shape((2,) + every, bf),
            shape((2, 4, 4, tokens, hidden), bf),
            shape((2, 4, 4, tokens, hidden), bf),
        ),
        in_specs=[vmem, vmem, hbm, hbm],
        out_specs=(vmem, vmem, hbm, hbm, hbm, hbm),
        scratch_shapes=[
            pltpu.VMEM(w_in.shape, bf),
            pltpu.VMEM(w_out.shape, bf),
            pltpu.VMEM(every, bf),
            pltpu.VMEM(every, bf),
            pltpu.VMEM((4, 4, tokens, hidden), bf),
            pltpu.VMEM((4, 4, tokens, hidden), bf),
            pltpu.VMEM((4, 4, tokens, width), fl),
            pltpu.VMEM((2, 4, 4, 4, tokens, width), bf),
            pltpu.VMEM((2, 4, 2, 2, tokens, width), bf),
            pltpu.VMEM((2, 4, 2, 4, tokens, width), bf),
            pltpu.VMEM((2,) + every, bf),
            pltpu.VMEM((2, 2, 2, tokens, features), bf),
            pltpu.VMEM((2, 2, 4, tokens, features), bf),
            pltpu.VMEM((2, 4, tokens, features), fl),
            pltpu.VMEM((2, 4, tokens, features), bf),
            pltpu.VMEM((2, 2, tokens // 2, features), bf),
            pltpu.VMEM((2, 2, tokens, features), bf),
            pltpu.SemaphoreType.DMA((N_SEMS,)),
        ],
        compiler_params=pltpu.CompilerParams(
            collective_id=1, has_side_effects=True, vmem_limit_bytes=60 * 2**20
        ),
    )(x, dy, w_in, w_out)


def contract_first(left, right):
    return lax.dot_general(
        left, right, (((0,), (0,)), ((), ())), preferred_element_type=jnp.float32
    )


def per_device(layer_input, w_in, w_out, output_grad):
    out, grad, x_all, dy_all, g_all, dh_all = run_block(layer_input, output_grad, w_in, w_out)
    features, hidden = w_in.shape
    w_in_grad = contract_first(x_all.reshape(-1, features), dh_all.reshape(-1, hidden))
    w_out_grad = contract_first(g_all.reshape(-1, hidden), dy_all.reshape(-1, features))
    return (b16(out), b16(grad), b16(w_in_grad), b16(w_out_grad))


def solution(mesh):
    in_specs = (
        P(("depth", "row"), "col"),
        P("col", "row"),
        P("row", "col"),
        P(("depth", "row"), "col"),
    )
    out_specs = (
        P(("depth", "row"), "col"),
        P(("depth", "row"), "col"),
        P("col", "row"),
        P("row", "col"),
    )
    return jax.shard_map(
        per_device, mesh=mesh, in_specs=in_specs, out_specs=out_specs, check_vma=False
    )
```

```python
import math

import jax
import jax.numpy as jnp
from jax import lax
from jax.experimental import pallas as pl
from jax.experimental.pallas import tpu as pltpu
from jax.sharding import PartitionSpec as P

MESH = pl.DeviceIdType.MESH
SIDE = 4
OWN, PREV, NEXT, FAR = range(4)
UNITS = (
    (
        ((OWN, 0, 3), (PREV, 0, 1), (NEXT, 0, 1)),
        ((OWN, 3, 4), (PREV, 1, 4), (NEXT, 1, 4), (FAR, 0, 4)),
    ),
    (((OWN, 0, 4), (PREV, 0, 4), (NEXT, 0, 4), (FAR, 0, 4)),),
)
SIZES = tuple(tuple(sum(hi - lo for _, lo, hi in unit) for unit in units) for units in UNITS)
STARTS = tuple(tuple(sum(sizes[:unit]) for unit in range(len(sizes))) for sizes in SIZES)
HALF = 16
LO, HI = pl.ds(0, 2), pl.ds(2, 2)
GROUPS = {"all": (OWN, 4), "others": (PREV, 3), "own": (OWN, 1)}
N_SEMS = 560


def gelu_parts(hidden):
    coeff = math.sqrt(2.0 / math.pi)
    square = hidden * hidden
    tangent = jnp.tanh(coeff * (hidden + 0.044715 * (square * hidden)))
    value = 0.5 * hidden * (1.0 + tangent)
    slope = 0.5 * (1.0 + tangent) + 0.5 * hidden * (1.0 - tangent * tangent) * coeff * (
        1.0 + 3.0 * 0.044715 * square
    )
    return (value, slope)


def f32(value):
    return value.astype(jnp.float32)


def b16(value):
    return value.astype(jnp.bfloat16)


class Ring:
    def __init__(self, after, before):
        self.after = after
        self.before = before


def block_kernel(
    x_ref, dy_ref, w_in_hbm, w_out_hbm,
    out_ref, grad_ref, x_hbm, dh_hbm, w_out_grad_hbm,
    w_in, w_out, x_all, dy_all, g_all, dh_all, slope, g_two, dy_two, w_out_grad,
    ysum, yfwd, yback, zsum, zfwd, zback, zown, xsum, xfwd, xback,
    sems,
):
    layer = lax.axis_index("depth")
    row = lax.axis_index("row")
    col = lax.axis_index("col")
    across, along = row // SIDE, row % SIDE

    def device(d, i, k, c):
        return (d, ((i + SIDE) % SIDE) * SIDE + (k + SIDE) % SIDE, (c + SIDE) % SIDE)

    ring_x = Ring(device(layer, across + 1, along, col), device(layer, across - 1, along, col))
    ring_z = Ring(device(layer, across, along + 1, col), device(layer, across, along - 1, col))
    ring_y = Ring(device(layer, across, along, col + 1), device(layer, across, along, col - 1))
    twin = (1 - layer, row, col)

    count = [0]
    sent = []

    def sem():
        count[0] += 1
        return sems.at[count[0] - 1]

    def send(src, dst, to):
        copy = pltpu.make_async_remote_copy(
            src_ref=src, dst_ref=dst, send_sem=sem(), recv_sem=sem(),
            device_id=to, device_id_type=MESH,
        )
        copy.start()
        sent.append(copy.wait_send)
        return copy

    def local(src, dst):
        copy = pltpu.make_async_copy(src, dst, sem())
        copy.start()
        return copy

    load_in = local(w_in_hbm, w_in)
    load_out = local(w_out_hbm, w_out)

    barrier = pltpu.get_barrier_semaphore()
    greeted = (ring_x.after, ring_x.before, ring_z.after, ring_z.before)
    greeted += (ring_y.after, ring_y.before, twin)
    for other in greeted:
        pl.semaphore_signal(barrier, inc=1, device_id=other, device_id_type=MESH)
    for half in range(2):
        rows = pl.ds(half * HALF, HALF)
        x_all[half, OWN, OWN] = x_ref[rows]
        dy_all[half, OWN, OWN] = dy_ref[rows]
    pl.semaphore_wait(barrier, len(greeted))

    kinds = ((x_all, ring_x, ring_z), (dy_all, ring_z, ring_x))
    features = x_all.shape[-1]
    left, right = pl.ds(0, features // 2), pl.ds(features // 2, features // 2)
    lines = {}
    planes = {}

    def share_block(kind, half, block):
        every, _, ring = kinds[kind]
        own = every.at[half, OWN, block]
        planes[kind, half, PREV, block] = send(own, every.at[half, PREV, block], ring.after)
        planes[kind, half, NEXT, block] = send(own, every.at[half, NEXT, block], ring.before)

    def open_line(kind, half):
        every, ring, _ = kinds[kind]
        own = every.at[half, OWN, OWN]
        lines[kind, half, PREV] = send(own, every.at[half, OWN, PREV], ring.after)
        lines[kind, half, NEXT] = send(own, every.at[half, OWN, NEXT], ring.before)

    def take_line(kind, half):
        every, ring, _ = kinds[kind]
        line = every.at[half, OWN]
        lines[kind, half, PREV].wait_recv()
        first = send(line.at[PREV, :, left], line.at[FAR, :, left], ring.after)
        lines[kind, half, NEXT].wait_recv()
        second = send(line.at[NEXT, :, right], line.at[FAR, :, right], ring.before)
        lines[kind, half, FAR] = (first, second)
        share_block(kind, half, PREV)
        share_block(kind, half, NEXT)

    def take_line_far(kind, half):
        for copy in lines[kind, half, FAR]:
            copy.wait_recv()
        share_block(kind, half, FAR)

    def take_block(kind, half, block):
        every, _, ring = kinds[kind]
        mine = every.at[half]
        planes[kind, half, PREV, block].wait_recv()
        if block in (OWN, PREV):
            copy = send(mine.at[PREV, block], mine.at[FAR, block], ring.after)
        planes[kind, half, NEXT, block].wait_recv()
        if block in (NEXT, FAR):
            copy = send(mine.at[NEXT, block], mine.at[FAR, block], ring.before)
        planes[kind, half, FAR, block] = copy

    def take_far(kind, half):
        for block in range(SIDE):
            planes[kind, half, FAR, block].wait_recv()

    for kind in range(2):
        open_line(kind, 0)
    for kind in range(2):
        share_block(kind, 0, OWN)

    width = slope.shape[-1]

    def rows_of(every, half, unit):
        parts = [every[half, plane, pl.ds(lo, hi - lo)] for plane, lo, hi in UNITS[half][unit]]
        part = parts[0] if len(parts) == 1 else jnp.concatenate(parts, axis=0)
        return part.reshape(part.shape[0] * part.shape[1], part.shape[2])

    def y_buffers(kind, half, unit):
        span = pl.ds(STARTS[half][unit], SIZES[half][unit])
        size = SIZES[half][unit]
        low, high = pl.ds(0, (size + 1) // 2), pl.ds((size + 1) // 2, size // 2)
        mine, fwd, back = ysum.at[kind, half, :, span], yfwd.at[kind, half], yback.at[kind, half]
        return mine, fwd.at[:, span], back.at[:, span], low, high

    sums = {}

    def y_product(kind, half, unit):
        mine, fwd, back, low, high = y_buffers(kind, half, unit)
        every = (x_all, dy_all)[kind]

        @pl.loop(0, 2)
        def _(tile):
            span = pl.ds(pl.multiple_of(tile * 2 * width, 2 * width), 2 * width)
            lhs = rows_of(every, half, unit)
            if kind == 0:
                part = jnp.dot(lhs, w_in[:, span], preferred_element_type=jnp.float32)
            else:
                part = lax.dot_general(
                    lhs, w_out[span, :], (((1,), (1,)), ((), ())),
                    preferred_element_type=jnp.float32,
                )
            part = b16(part)
            for piece in range(2):
                shard = (2 * tile + piece + SIDE - col) % SIDE
                cut = part[:, piece * width : (piece + 1) * width]
                mine[shard] = cut.reshape(SIZES[half][unit], HALF, width)

        sums[kind, half, unit] = [
            send(mine.at[2, high], fwd.at[0, high], ring_y.after),
            send(mine.at[2, low], fwd.at[1, low], ring_y.before),
            send(mine.at[1, low], back.at[0, low], ring_y.after),
            send(mine.at[3, high], back.at[1, high], ring_y.before),
        ]

    def y_relay(kind, half, unit):
        mine, fwd, back, low, high = y_buffers(kind, half, unit)
        copies = sums[kind, half, unit]
        copies[0].wait_recv()
        mine[1, high] = b16(f32(mine[1, high]) + f32(fwd[0, high]))
        copies.append(send(mine.at[1, high], back.at[0, high], ring_y.after))
        copies[1].wait_recv()
        mine[3, low] = b16(f32(mine[3, low]) + f32(fwd[1, low]))
        copies.append(send(mine.at[3, low], back.at[1, low], ring_y.before))

    def y_total(kind, half, unit):
        for copy in sums[kind, half, unit][2:]:
            copy.wait_recv()
        mine, _, back, _, _ = y_buffers(kind, half, unit)
        return f32(mine[0]) + f32(back[0]) + f32(back[1])

    own_columns = pl.ds(pl.multiple_of(col * width, width), width)

    def finish_hidden(half, unit):
        value, steep = gelu_parts(y_total(0, half, unit))
        value = b16(value)
        at = 0
        for plane, lo, hi in UNITS[half][unit]:
            span = pl.ds(lo, hi - lo)
            g_all[half, plane, span, :, own_columns] = value[at : at + hi - lo]
            slope[half, plane, span] = steep[at : at + hi - lo]
            at += hi - lo

    def finish_grad(half):
        for unit, pieces in enumerate(UNITS[half]):
            total = y_total(1, half, unit)
            at = 0
            for plane, lo, hi in pieces:
                for block in range(lo, hi):
                    part = b16(total[at] * slope[half, block, plane])
                    dh_all[half, plane, block, :, own_columns] = part
                    at += 1

    keep = []
    shared = []

    def share(src, dst):
        keep.append(local(src, dst))
        shared.append(send(src, dst, twin))

    def share_inputs(half):
        share(x_all.at[half], x_hbm.at[layer, half])
        for plane in range(SIDE):
            share(dy_all.at[half, plane], dy_two.at[layer, half, :, plane])

    def group_of(kind, half, group):
        first, size = GROUPS[group]
        return (g_all, dh_all)[kind].at[half, pl.ds(first, size)]

    def columns_of(step):
        at = (col + step + SIDE) % SIDE
        return pl.ds(pl.multiple_of(at * width, width), width)

    passes = {}

    def start(kind, half, group):
        own = group_of(kind, half, group).at[:, :, :, own_columns]
        passes[kind, half, group] = [send(own, own, ring_y.after), send(own, own, ring_y.before)]

    def relay(kind, half, group):
        copies, every = passes[kind, half, group], group_of(kind, half, group)
        copies[0].wait_recv()
        part = every.at[:, LO, :, columns_of(-1)]
        copies.append(send(part, part, ring_y.after))
        copies[1].wait_recv()
        part = every.at[:, HI, :, columns_of(1)]
        copies.append(send(part, part, ring_y.before))

    def product(kind, half, group):
        first, size = GROUPS[group]
        every = (g_all, dh_all)[kind]

        @pl.loop(0, 4)
        def _(tile):
            cols = w_out.shape[1] // 4
            span = pl.ds(pl.multiple_of(tile * cols, cols), cols)
            lhs = every[half, pl.ds(first, size)].reshape(-1, every.shape[-1])
            if kind == 0:
                part = jnp.dot(lhs, w_out[:, span], preferred_element_type=jnp.float32)
            else:
                part = lax.dot_general(
                    lhs, w_in[span, :], (((1,), (1,)), ((), ())),
                    preferred_element_type=jnp.float32,
                )
            part = part.reshape(size, SIDE, HALF, cols)
            if first == OWN:
                zown[kind, half, :, :, span] = part[0]
                part = part[1:]
            if size > 1:
                zsum[kind, half, pl.ds(1, 3), :, :, span] = b16(part)

    moves = {}
    plane_rings = (ring_z, ring_x)
    block_rings = (ring_x, ring_z)

    def planes_start(kind, half):
        ring = plane_rings[kind]
        mine, fwd, back = zsum.at[kind, half], zfwd.at[kind, half], zback.at[kind, half]
        moves[kind, half, FAR] = (
            send(mine.at[FAR, HI], fwd.at[0], ring.after),
            send(mine.at[FAR, LO], fwd.at[1], ring.before),
        )
        moves[kind, half, OWN] = [
            send(mine.at[NEXT, LO], back.at[0, LO], ring.after),
            send(mine.at[PREV, HI], back.at[1, HI], ring.before),
        ]

    def planes_relay(kind, half):
        ring = plane_rings[kind]
        mine, fwd, back = zsum.at[kind, half], zfwd.at[kind, half], zback.at[kind, half]
        moves[kind, half, FAR][0].wait_recv()
        mine[NEXT, HI] = b16(f32(mine[NEXT, HI]) + f32(fwd[0]))
        moves[kind, half, OWN].append(send(mine.at[NEXT, HI], back.at[0, HI], ring.after))
        moves[kind, half, FAR][1].wait_recv()
        mine[PREV, LO] = b16(f32(mine[PREV, LO]) + f32(fwd[1]))
        moves[kind, half, OWN].append(send(mine.at[PREV, LO], back.at[1, LO], ring.before))

    lasts = {}

    def blocks_start(kind, half):
        ring = block_rings[kind]
        for copy in moves[kind, half, OWN]:
            copy.wait_recv()
        own, others = zown.at[kind, half], zback.at[kind, half]
        mine, fwd, back = xsum.at[kind, half], xfwd.at[kind, half], xback.at[kind, half]
        for block in (FAR, NEXT, PREV, OWN):
            total = own[block] + f32(others[0, block]) + f32(others[1, block])
            if block == OWN:
                own[OWN] = total
            else:
                mine[block] = b16(total)
        lasts[kind, half] = [
            send(mine.at[FAR, :, right], fwd.at[0], ring.after),
            send(mine.at[FAR, :, left], fwd.at[1], ring.before),
            send(mine.at[NEXT, :, left], back.at[0, :, left], ring.after),
            send(mine.at[PREV, :, right], back.at[1, :, right], ring.before),
        ]

    def blocks_relay(kind, half):
        ring, copies = block_rings[kind], lasts[kind, half]
        mine, fwd, back = xsum.at[kind, half], xfwd.at[kind, half], xback.at[kind, half]
        copies[0].wait_recv()
        mine[NEXT, :, right] = b16(f32(mine[NEXT, :, right]) + f32(fwd[0]))
        copies.append(send(mine.at[NEXT, :, right], back.at[0, :, right], ring.after))
        copies[1].wait_recv()
        mine[PREV, :, left] = b16(f32(mine[PREV, :, left]) + f32(fwd[1]))
        copies.append(send(mine.at[PREV, :, left], back.at[1, :, left], ring.before))

    def blocks_total(kind, half):
        for copy in lasts[kind, half][2:]:
            copy.wait_recv()
        rows = pl.ds(half * HALF, HALF)
        own, back = zown.at[kind, half], xback.at[kind, half]
        total = f32((x_ref, dy_ref)[kind][rows]) + own[OWN] + f32(back[0]) + f32(back[1])
        (out_ref, grad_ref)[kind][rows] = b16(total)

    def finish(kind, half, group):
        for copy in passes[kind, half, group][2:]:
            copy.wait_recv()
        first, size = GROUPS[group]
        if kind == 0:
            span = pl.ds(first, size)
            share(g_all.at[half, span], g_two.at[layer, half, span])
        else:
            for plane in range(first, first + size):
                share(dh_all.at[half, plane], dh_hbm.at[layer, half, :, plane])
        product(kind, half, group)
        if size > 1:
            planes_start(kind, half)

    def settle():
        for copy in keep:
            copy.wait()
        for copy in shared:
            copy.wait_recv()
        keep.clear()
        shared.clear()

    def out_gradient(tile):
        rows = 512
        span = pl.ds(tile * rows, rows)

        @pl.loop(0, 2)
        def _(side):
            cols = dy_two.shape[-1] // 2
            part = pl.ds(pl.multiple_of(side * cols, cols), cols)
            lhs = g_two[:, :, :, :, :, span].reshape(-1, rows)
            rhs = dy_two[:, :, :, :, :, part].reshape(-1, cols)
            total = lax.dot_general(
                lhs, rhs, (((0,), (0,)), ((), ())), preferred_element_type=jnp.float32
            )
            w_out_grad[span, part] = b16(total)

        keep.append(local(w_out_grad.at[span], w_out_grad_hbm.at[span]))

    for kind in range(2):
        take_line(kind, 0)
    for kind in range(2):
        take_block(kind, 0, OWN)
    load_in.wait()
    y_product(0, 0, 0)
    for kind in range(2):
        take_line_far(kind, 0)
    load_out.wait()
    y_product(1, 0, 0)
    for kind in range(2):
        open_line(kind, 1)
        share_block(kind, 1, OWN)
    for kind in range(2):
        take_block(kind, 0, PREV)
        take_block(kind, 0, NEXT)
    y_relay(0, 0, 0)
    y_relay(1, 0, 0)
    for kind in range(2):
        take_block(kind, 0, FAR)
    for kind in range(2):
        take_line(kind, 1)
    for kind in range(2):
        take_far(kind, 0)
    y_product(0, 0, 1)
    y_product(1, 0, 1)
    finish_hidden(0, 0)
    for kind in range(2):
        take_block(kind, 1, OWN)
        take_line_far(kind, 1)
    y_relay(0, 0, 1)
    for kind in range(2):
        take_block(kind, 1, PREV)
        take_block(kind, 1, NEXT)
    y_relay(1, 0, 1)
    finish_hidden(0, 1)
    start(0, 0, "all")
    for kind in range(2):
        take_block(kind, 1, FAR)
    finish_grad(0)
    start(1, 0, "all")
    for kind in range(2):
        take_far(kind, 1)
    y_product(0, 1, 0)
    relay(0, 0, "all")
    y_product(1, 1, 0)
    relay(1, 0, "all")
    y_relay(0, 1, 0)
    finish(0, 0, "all")
    y_relay(1, 1, 0)
    finish(1, 0, "all")
    finish_hidden(1, 0)
    start(0, 1, "others")
    finish_grad(1)
    start(1, 1, "others")
    planes_relay(0, 0)
    planes_relay(1, 0)
    relay(0, 1, "others")
    start(0, 1, "own")
    relay(1, 1, "others")
    start(1, 1, "own")
    finish(0, 1, "others")
    relay(0, 1, "own")
    blocks_start(0, 0)
    finish(1, 1, "others")
    relay(1, 1, "own")
    blocks_start(1, 0)
    share_inputs(0)
    share_inputs(1)
    finish(0, 1, "own")
    planes_relay(0, 1)
    blocks_relay(0, 0)
    finish(1, 1, "own")
    planes_relay(1, 1)
    blocks_relay(1, 0)
    settle()
    out_gradient(0)
    blocks_start(0, 1)
    blocks_start(1, 1)
    blocks_total(0, 0)
    blocks_total(1, 0)
    out_gradient(1)
    blocks_relay(0, 1)
    blocks_relay(1, 1)
    out_gradient(2)
    blocks_total(0, 1)
    blocks_total(1, 1)

    for copy in keep:
        copy.wait()
    for copy in shared:
        copy.wait_recv()
    for wait_send in sent:
        wait_send()


def run_block(x, dy, w_in, w_out):
    tokens, features = x.shape
    hidden = w_in.shape[1]
    width = hidden // SIDE
    held = (2, SIDE, SIDE, HALF)
    bf, fl = jnp.bfloat16, jnp.float32
    vmem = pl.BlockSpec(memory_space=pltpu.VMEM)
    hbm = pl.BlockSpec(memory_space=pl.ANY)
    shape = jax.ShapeDtypeStruct
    return pl.pallas_call(
        block_kernel,
        out_shape=(
            shape((tokens, features), bf),
            shape((tokens, features), bf),
            shape((2,) + held + (features,), bf),
            shape((2,) + held + (hidden,), bf),
            shape(w_out.shape, bf),
        ),
        in_specs=[vmem, vmem, hbm, hbm],
        out_specs=(vmem, vmem, hbm, hbm, hbm),
        scratch_shapes=[
            pltpu.VMEM(w_in.shape, bf),
            pltpu.VMEM(w_out.shape, bf),
            pltpu.VMEM(held + (features,), bf),
            pltpu.VMEM(held + (features,), bf),
            pltpu.VMEM(held + (hidden,), bf),
            pltpu.VMEM(held + (hidden,), bf),
            pltpu.VMEM(held + (width,), fl),
            pltpu.VMEM((2,) + held + (hidden,), bf),
            pltpu.VMEM((2,) + held + (features,), bf),
            pltpu.VMEM(w_out.shape, bf),
            pltpu.VMEM((2, 2, SIDE, 16, HALF, width), bf),
            pltpu.VMEM((2, 2, 2, 16, HALF, width), bf),
            pltpu.VMEM((2, 2, 2, 16, HALF, width), bf),
            pltpu.VMEM((2, 2, SIDE, SIDE, HALF, features), bf),
            pltpu.VMEM((2, 2, 2, 2, HALF, features), bf),
            pltpu.VMEM((2, 2, 2, SIDE, HALF, features), bf),
            pltpu.VMEM((2, 2, SIDE, HALF, features), fl),
            pltpu.VMEM((2, 2, SIDE, HALF, features), bf),
            pltpu.VMEM((2, 2, 2, HALF, features // 2), bf),
            pltpu.VMEM((2, 2, 2, HALF, features), bf),
            pltpu.SemaphoreType.DMA((N_SEMS,)),
        ],
        compiler_params=pltpu.CompilerParams(
            collective_id=1, has_side_effects=True, vmem_limit_bytes=60 * 2**20
        ),
    )(x, dy, w_in, w_out)


def grads_kernel(x_ref, dh_ref, kept_ref, out_ref, grad_ref, w_in_grad, w_out_grad, out, grad):
    part = lax.dot_general(
        x_ref[...], dh_ref[...], (((0,), (0,)), ((), ())), preferred_element_type=jnp.float32
    )
    w_in_grad[...] = b16(part)
    w_out_grad[...] = kept_ref[...]

    @pl.when(pl.program_id(0) == 0)
    def _():
        out[...] = out_ref[...]
        grad[...] = grad_ref[...]


def per_device(layer_input, w_in, w_out, output_grad):
    out, grad, x_two, dh_two, kept = run_block(layer_input, output_grad, w_in, w_out)
    features, hidden = w_in.shape
    x_two, dh_two = x_two.reshape(-1, features), dh_two.reshape(-1, hidden)
    tokens, steps = x_two.shape[0], 4
    small = pl.BlockSpec(out.shape, lambda i: (0, 0))
    wide = pl.BlockSpec((features // steps, hidden), lambda i: (i, 0))
    tall = pl.BlockSpec((hidden // steps, features), lambda i: (i, 0))
    bf = jnp.bfloat16
    w_in_grad, w_out_grad, out, grad = pl.pallas_call(
        grads_kernel,
        grid=(steps,),
        out_shape=[jax.ShapeDtypeStruct(a.shape, bf) for a in (w_in, w_out, out, grad)],
        in_specs=[
            pl.BlockSpec((tokens, features // steps), lambda i: (0, i)),
            pl.BlockSpec((tokens, hidden), lambda i: (0, 0)),
            tall,
            small,
            small,
        ],
        out_specs=[wide, tall, small, small],
        compiler_params=pltpu.CompilerParams(vmem_limit_bytes=60 * 2**20),
    )(x_two, dh_two, kept, out, grad)
    return (out, grad, w_in_grad, w_out_grad)


def solution(mesh):
    in_specs = (
        P(("depth", "row"), "col"),
        P("col", "row"),
        P("row", "col"),
        P(("depth", "row"), "col"),
    )
    out_specs = (
        P(("depth", "row"), "col"),
        P(("depth", "row"), "col"),
        P("col", "row"),
        P("row", "col"),
    )
    return jax.shard_map(
        per_device, mesh=mesh, in_specs=in_specs, out_specs=out_specs, check_vma=False
    )
```

```python
import math

import jax
import jax.numpy as jnp
from jax import lax
from jax.experimental import pallas as pl
from jax.experimental.pallas import tpu as pltpu
from jax.sharding import PartitionSpec as P

MESH = pl.DeviceIdType.MESH
SIDE = 4
OWN, PREV, NEXT, FAR = range(4)
UNITS = (
    (
        ((OWN, 0, 3), (PREV, 0, 1), (NEXT, 0, 1)),
        ((OWN, 3, 4), (PREV, 1, 4), (NEXT, 1, 4), (FAR, 0, 4)),
    ),
    (((OWN, 0, 4), (PREV, 0, 4), (NEXT, 0, 4), (FAR, 0, 4)),),
)
SIZES = tuple(tuple(sum(hi - lo for _, lo, hi in unit) for unit in units) for units in UNITS)
STARTS = tuple(tuple(sum(sizes[:unit]) for unit in range(len(sizes))) for sizes in SIZES)
HALF = 16
LO, HI = pl.ds(0, 2), pl.ds(2, 2)
BOTH = 2
GROUPS = {"others": (PREV, 3), "own": (OWN, 1)}
N_SEMS = 560


def gelu_parts(hidden):
    coeff = math.sqrt(2.0 / math.pi)
    square = hidden * hidden
    tangent = jnp.tanh(coeff * (hidden + 0.044715 * (square * hidden)))
    value = 0.5 * hidden * (1.0 + tangent)
    slope = 0.5 * (1.0 + tangent) + 0.5 * hidden * (1.0 - tangent * tangent) * coeff * (
        1.0 + 3.0 * 0.044715 * square
    )
    return (value, slope)


def f32(value):
    return value.astype(jnp.float32)


def b16(value):
    return value.astype(jnp.bfloat16)


class Ring:
    def __init__(self, after, before):
        self.after = after
        self.before = before


def block_kernel(
    x_ref, dy_ref, w_in_hbm, w_out_hbm,
    out_ref, grad_ref, x_hbm, dh_hbm, w_out_grad_hbm,
    w_in, w_out, x_all, dy_all, g_all, dh_all, slope, g_two, dy_two, w_out_grad,
    ysum, yfwd, yback, zsum, zfwd, zback, zown, xsum, xfwd, xback,
    sems,
):
    layer = lax.axis_index("depth")
    row = lax.axis_index("row")
    col = lax.axis_index("col")
    across, along = row // SIDE, row % SIDE

    def device(d, i, k, c):
        return (d, ((i + SIDE) % SIDE) * SIDE + (k + SIDE) % SIDE, (c + SIDE) % SIDE)

    ring_x = Ring(device(layer, across + 1, along, col), device(layer, across - 1, along, col))
    ring_z = Ring(device(layer, across, along + 1, col), device(layer, across, along - 1, col))
    ring_y = Ring(device(layer, across, along, col + 1), device(layer, across, along, col - 1))
    twin = (1 - layer, row, col)

    count = [0]
    sent = []

    def sem():
        count[0] += 1
        return sems.at[count[0] - 1]

    def send(src, dst, to):
        copy = pltpu.make_async_remote_copy(
            src_ref=src, dst_ref=dst, send_sem=sem(), recv_sem=sem(),
            device_id=to, device_id_type=MESH,
        )
        copy.start()
        sent.append(copy.wait_send)
        return copy

    def local(src, dst):
        copy = pltpu.make_async_copy(src, dst, sem())
        copy.start()
        return copy

    load_in = local(w_in_hbm, w_in)
    load_out = local(w_out_hbm, w_out)

    barrier = pltpu.get_barrier_semaphore()
    greeted = (ring_x.after, ring_x.before, ring_z.after, ring_z.before)
    greeted += (ring_y.after, ring_y.before, twin)
    for other in greeted:
        pl.semaphore_signal(barrier, inc=1, device_id=other, device_id_type=MESH)
    for half in range(2):
        rows = pl.ds(half * HALF, HALF)
        x_all[half, OWN, OWN] = x_ref[rows]
        dy_all[half, OWN, OWN] = dy_ref[rows]
    pl.semaphore_wait(barrier, len(greeted))

    kinds = ((x_all, ring_x, ring_z), (dy_all, ring_z, ring_x))
    features = x_all.shape[-1]
    left, right = pl.ds(0, features // 2), pl.ds(features // 2, features // 2)
    lines = {}
    planes = {}

    def share_block(kind, half, block):
        every, _, ring = kinds[kind]
        own = every.at[half, OWN, block]
        planes[kind, half, PREV, block] = send(own, every.at[half, PREV, block], ring.after)
        planes[kind, half, NEXT, block] = send(own, every.at[half, NEXT, block], ring.before)

    def open_line(kind, half):
        every, ring, _ = kinds[kind]
        own = every.at[half, OWN, OWN]
        lines[kind, half, PREV] = send(own, every.at[half, OWN, PREV], ring.after)
        lines[kind, half, NEXT] = send(own, every.at[half, OWN, NEXT], ring.before)

    def take_line(kind, half):
        every, ring, _ = kinds[kind]
        line = every.at[half, OWN]
        lines[kind, half, PREV].wait_recv()
        first = send(line.at[PREV, :, left], line.at[FAR, :, left], ring.after)
        lines[kind, half, NEXT].wait_recv()
        second = send(line.at[NEXT, :, right], line.at[FAR, :, right], ring.before)
        lines[kind, half, FAR] = (first, second)
        share_block(kind, half, PREV)
        share_block(kind, half, NEXT)

    def take_line_far(kind, half):
        for copy in lines[kind, half, FAR]:
            copy.wait_recv()
        share_block(kind, half, FAR)

    def take_block(kind, half, block):
        every, _, ring = kinds[kind]
        mine = every.at[half]
        planes[kind, half, PREV, block].wait_recv()
        if block in (OWN, PREV):
            copy = send(mine.at[PREV, block], mine.at[FAR, block], ring.after)
        planes[kind, half, NEXT, block].wait_recv()
        if block in (NEXT, FAR):
            copy = send(mine.at[NEXT, block], mine.at[FAR, block], ring.before)
        planes[kind, half, FAR, block] = copy

    def take_far(kind, half):
        for block in range(SIDE):
            planes[kind, half, FAR, block].wait_recv()

    for kind in range(2):
        open_line(kind, 0)
    for kind in range(2):
        share_block(kind, 0, OWN)

    width = slope.shape[-1]

    def rows_of(every, half, unit):
        parts = [every[half, plane, pl.ds(lo, hi - lo)] for plane, lo, hi in UNITS[half][unit]]
        part = parts[0] if len(parts) == 1 else jnp.concatenate(parts, axis=0)
        return part.reshape(part.shape[0] * part.shape[1], part.shape[2])

    def y_buffers(kind, half, unit):
        span = pl.ds(STARTS[half][unit], SIZES[half][unit])
        size = SIZES[half][unit]
        low, high = pl.ds(0, (size + 1) // 2), pl.ds((size + 1) // 2, size // 2)
        mine, fwd, back = ysum.at[kind, half, :, span], yfwd.at[kind, half], yback.at[kind, half]
        return mine, fwd.at[:, span], back.at[:, span], low, high

    sums = {}

    def y_product(kind, half, unit):
        mine, fwd, back, low, high = y_buffers(kind, half, unit)
        every = (x_all, dy_all)[kind]

        @pl.loop(0, 2)
        def _(tile):
            span = pl.ds(pl.multiple_of(tile * 2 * width, 2 * width), 2 * width)
            lhs = rows_of(every, half, unit)
            if kind == 0:
                part = jnp.dot(lhs, w_in[:, span], preferred_element_type=jnp.float32)
            else:
                part = lax.dot_general(
                    lhs, w_out[span, :], (((1,), (1,)), ((), ())),
                    preferred_element_type=jnp.float32,
                )
            part = b16(part)
            for piece in range(2):
                shard = (2 * tile + piece + SIDE - col) % SIDE
                cut = part[:, piece * width : (piece + 1) * width]
                mine[shard] = cut.reshape(SIZES[half][unit], HALF, width)

        sums[kind, half, unit] = [
            send(mine.at[2, high], fwd.at[0, high], ring_y.after),
            send(mine.at[2, low], fwd.at[1, low], ring_y.before),
            send(mine.at[1, low], back.at[0, low], ring_y.after),
            send(mine.at[3, high], back.at[1, high], ring_y.before),
        ]

    def y_relay(kind, half, unit):
        mine, fwd, back, low, high = y_buffers(kind, half, unit)
        copies = sums[kind, half, unit]
        copies[0].wait_recv()
        mine[1, high] = b16(f32(mine[1, high]) + f32(fwd[0, high]))
        copies.append(send(mine.at[1, high], back.at[0, high], ring_y.after))
        copies[1].wait_recv()
        mine[3, low] = b16(f32(mine[3, low]) + f32(fwd[1, low]))
        copies.append(send(mine.at[3, low], back.at[1, low], ring_y.before))

    def y_total(kind, half, unit):
        for copy in sums[kind, half, unit][2:]:
            copy.wait_recv()
        mine, _, back, _, _ = y_buffers(kind, half, unit)
        return f32(mine[0]) + f32(back[0]) + f32(back[1])

    own_columns = pl.ds(pl.multiple_of(col * width, width), width)

    def finish_hidden(half, unit):
        value, steep = gelu_parts(y_total(0, half, unit))
        value = b16(value)
        at = 0
        for plane, lo, hi in UNITS[half][unit]:
            span = pl.ds(lo, hi - lo)
            g_all[half, plane, span, :, own_columns] = value[at : at + hi - lo]
            slope[half, plane, span] = steep[at : at + hi - lo]
            at += hi - lo

    def finish_grad(half):
        for unit, pieces in enumerate(UNITS[half]):
            total = y_total(1, half, unit)
            at = 0
            for plane, lo, hi in pieces:
                for block in range(lo, hi):
                    part = b16(total[at] * slope[half, block, plane])
                    dh_all[half, plane, block, :, own_columns] = part
                    at += 1

    keep = []
    shared = []

    def share(src, dst):
        keep.append(local(src, dst))
        shared.append(send(src, dst, twin))

    def share_inputs(half):
        share(x_all.at[half], x_hbm.at[layer, half])
        for plane in range(SIDE):
            share(dy_all.at[half, plane], dy_two.at[layer, half, :, plane])

    def group_of(kind, half, group):
        first, size = GROUPS[group]
        every = (g_all, dh_all)[kind]
        if half == BOTH:
            return every.at[:, first]
        return every.at[half, pl.ds(first, size)]

    def columns_of(step):
        at = (col + step + SIDE) % SIDE
        return pl.ds(pl.multiple_of(at * width, width), width)

    passes = {}

    def start(kind, half, group):
        own = group_of(kind, half, group).at[:, :, :, own_columns]
        passes[kind, half, group] = [send(own, own, ring_y.after), send(own, own, ring_y.before)]

    def relay(kind, half, group):
        copies, every = passes[kind, half, group], group_of(kind, half, group)
        copies[0].wait_recv()
        part = every.at[:, LO, :, columns_of(-1)]
        copies.append(send(part, part, ring_y.after))
        copies[1].wait_recv()
        part = every.at[:, HI, :, columns_of(1)]
        copies.append(send(part, part, ring_y.before))

    def product(kind, half, group):
        first, size = GROUPS[group]
        every = (g_all, dh_all)[kind]

        @pl.loop(0, 4)
        def _(tile):
            cols = w_out.shape[1] // 4
            span = pl.ds(pl.multiple_of(tile * cols, cols), cols)
            lhs = every[:, first] if half == BOTH else every[half, pl.ds(first, size)]
            lhs = lhs.reshape(-1, every.shape[-1])
            if kind == 0:
                part = jnp.dot(lhs, w_out[:, span], preferred_element_type=jnp.float32)
            else:
                part = lax.dot_general(
                    lhs, w_in[span, :], (((1,), (1,)), ((), ())),
                    preferred_element_type=jnp.float32,
                )
            part = part.reshape(-1, SIDE, HALF, cols)
            if half == BOTH:
                zown[kind, :, :, :, span] = part
            else:
                zsum[kind, half, pl.ds(first, size), :, :, span] = b16(part)

    moves = {}
    plane_rings = (ring_z, ring_x)
    block_rings = (ring_x, ring_z)

    def planes_start(kind, half):
        ring = plane_rings[kind]
        mine, fwd, back = zsum.at[kind, half], zfwd.at[kind, half], zback.at[kind, half]
        moves[kind, half, FAR] = (
            send(mine.at[FAR, HI], fwd.at[0], ring.after),
            send(mine.at[FAR, LO], fwd.at[1], ring.before),
        )
        moves[kind, half, OWN] = [
            send(mine.at[NEXT, LO], back.at[0, LO], ring.after),
            send(mine.at[PREV, HI], back.at[1, HI], ring.before),
        ]

    def planes_relay(kind, half):
        ring = plane_rings[kind]
        mine, fwd, back = zsum.at[kind, half], zfwd.at[kind, half], zback.at[kind, half]
        moves[kind, half, FAR][0].wait_recv()
        mine[NEXT, HI] = b16(f32(mine[NEXT, HI]) + f32(fwd[0]))
        moves[kind, half, OWN].append(send(mine.at[NEXT, HI], back.at[0, HI], ring.after))
        moves[kind, half, FAR][1].wait_recv()
        mine[PREV, LO] = b16(f32(mine[PREV, LO]) + f32(fwd[1]))
        moves[kind, half, OWN].append(send(mine.at[PREV, LO], back.at[1, LO], ring.before))

    lasts = {}

    def blocks_start(kind, half):
        ring = block_rings[kind]
        for copy in moves[kind, half, OWN]:
            copy.wait_recv()
        own, others = zown.at[kind, half], zback.at[kind, half]
        mine, fwd, back = xsum.at[kind, half], xfwd.at[kind, half], xback.at[kind, half]
        for block in (FAR, NEXT, PREV, OWN):
            total = own[block] + f32(others[0, block]) + f32(others[1, block])
            if block == OWN:
                own[OWN] = total
            else:
                mine[block] = b16(total)
        lasts[kind, half] = [
            send(mine.at[FAR, :, right], fwd.at[0], ring.after),
            send(mine.at[FAR, :, left], fwd.at[1], ring.before),
            send(mine.at[NEXT, :, left], back.at[0, :, left], ring.after),
            send(mine.at[PREV, :, right], back.at[1, :, right], ring.before),
        ]

    def blocks_relay(kind, half):
        ring, copies = block_rings[kind], lasts[kind, half]
        mine, fwd, back = xsum.at[kind, half], xfwd.at[kind, half], xback.at[kind, half]
        copies[0].wait_recv()
        mine[NEXT, :, right] = b16(f32(mine[NEXT, :, right]) + f32(fwd[0]))
        copies.append(send(mine.at[NEXT, :, right], back.at[0, :, right], ring.after))
        copies[1].wait_recv()
        mine[PREV, :, left] = b16(f32(mine[PREV, :, left]) + f32(fwd[1]))
        copies.append(send(mine.at[PREV, :, left], back.at[1, :, left], ring.before))

    def blocks_total(kind, half):
        for copy in lasts[kind, half][2:]:
            copy.wait_recv()
        rows = pl.ds(half * HALF, HALF)
        own, back = zown.at[kind, half], xback.at[kind, half]
        total = f32((x_ref, dy_ref)[kind][rows]) + own[OWN] + f32(back[0]) + f32(back[1])
        (out_ref, grad_ref)[kind][rows] = b16(total)

    def finish(kind, half, group):
        for copy in passes[kind, half, group][2:]:
            copy.wait_recv()
        first, size = GROUPS[group]
        for each in range(2) if half == BOTH else (half,):
            if kind == 0:
                span = pl.ds(first, size)
                share(g_all.at[each, span], g_two.at[layer, each, span])
            else:
                for plane in range(first, first + size):
                    share(dh_all.at[each, plane], dh_hbm.at[layer, each, :, plane])
        product(kind, half, group)
        if half != BOTH:
            planes_start(kind, half)

    def settle():
        for copy in keep:
            copy.wait()
        for copy in shared:
            copy.wait_recv()
        keep.clear()
        shared.clear()

    def out_gradient(tile):
        rows = 512
        span = pl.ds(tile * rows, rows)

        @pl.loop(0, 2)
        def _(side):
            cols = dy_two.shape[-1] // 2
            part = pl.ds(pl.multiple_of(side * cols, cols), cols)
            lhs = g_two[:, :, :, :, :, span].reshape(-1, rows)
            rhs = dy_two[:, :, :, :, :, part].reshape(-1, cols)
            total = lax.dot_general(
                lhs, rhs, (((0,), (0,)), ((), ())), preferred_element_type=jnp.float32
            )
            w_out_grad[span, part] = b16(total)

        keep.append(local(w_out_grad.at[span], w_out_grad_hbm.at[span]))

    take_line(0, 0)
    load_in.wait()
    take_line(1, 0)
    take_line_far(0, 0)
    take_block(1, 0, OWN)
    take_block(0, 0, OWN)
    y_product(0, 0, 0)
    take_block(0, 0, NEXT)
    load_out.wait()
    open_line(0, 1)
    take_line_far(1, 0)
    take_block(0, 0, FAR)
    take_block(0, 0, PREV)
    y_relay(0, 0, 0)
    take_block(1, 0, NEXT)
    take_block(1, 0, PREV)
    y_product(1, 0, 0)
    open_line(1, 1)
    take_block(1, 0, FAR)
    share_block(0, 1, OWN)
    take_far(0, 0)
    y_product(0, 0, 1)
    take_far(1, 0)
    take_line(0, 1)
    y_product(1, 0, 1)
    take_line_far(0, 1)
    y_relay(0, 0, 1)
    take_line(1, 1)
    finish_hidden(0, 0)
    take_block(0, 1, FAR)
    share_block(1, 1, OWN)
    y_relay(1, 0, 0)
    y_relay(1, 0, 1)
    take_block(0, 1, PREV)
    take_block(0, 1, OWN)
    take_block(0, 1, NEXT)
    finish_hidden(0, 1)
    start(0, 0, "others")
    take_line_far(1, 1)
    finish_grad(0)
    start(1, 0, "others")
    take_far(0, 1)
    take_block(1, 1, PREV)
    take_block(1, 1, NEXT)
    take_block(1, 1, FAR)
    y_product(0, 1, 0)
    relay(0, 0, "others")
    take_block(1, 1, OWN)
    take_far(1, 1)
    y_product(1, 1, 0)
    y_relay(0, 1, 0)
    finish(0, 0, "others")
    share_inputs(1)
    relay(1, 0, "others")
    y_relay(1, 1, 0)
    finish_hidden(1, 0)
    start(0, 1, "others")
    finish_grad(1)
    start(1, 1, "others")
    finish(1, 0, "others")
    relay(0, 1, "others")
    relay(1, 1, "others")
    planes_relay(0, 0)
    share_inputs(0)
    start(1, BOTH, "own")
    finish(0, 1, "others")
    planes_relay(1, 0)
    start(0, BOTH, "own")
    finish(1, 1, "others")
    relay(1, BOTH, "own")
    relay(0, BOTH, "own")
    planes_relay(0, 1)
    finish(1, BOTH, "own")
    blocks_start(1, 0)
    planes_relay(1, 1)
    finish(0, BOTH, "own")
    settle()
    blocks_start(0, 1)
    out_gradient(1)
    blocks_start(0, 0)
    blocks_start(1, 1)
    blocks_relay(0, 1)
    out_gradient(2)
    blocks_relay(1, 0)
    blocks_relay(0, 0)
    blocks_relay(1, 1)
    out_gradient(0)
    blocks_total(1, 0)
    blocks_total(0, 1)
    blocks_total(0, 0)
    blocks_total(1, 1)

    for copy in keep:
        copy.wait()
    for copy in shared:
        copy.wait_recv()
    for wait_send in sent:
        wait_send()


def run_block(x, dy, w_in, w_out):
    tokens, features = x.shape
    hidden = w_in.shape[1]
    width = hidden // SIDE
    held = (2, SIDE, SIDE, HALF)
    bf, fl = jnp.bfloat16, jnp.float32
    vmem = pl.BlockSpec(memory_space=pltpu.VMEM)
    hbm = pl.BlockSpec(memory_space=pl.ANY)
    shape = jax.ShapeDtypeStruct
    return pl.pallas_call(
        block_kernel,
        out_shape=(
            shape((tokens, features), bf),
            shape((tokens, features), bf),
            shape((2,) + held + (features,), bf),
            shape((2,) + held + (hidden,), bf),
            shape(w_out.shape, bf),
        ),
        in_specs=[vmem, vmem, hbm, hbm],
        out_specs=(vmem, vmem, hbm, hbm, hbm),
        scratch_shapes=[
            pltpu.VMEM(w_in.shape, bf),
            pltpu.VMEM(w_out.shape, bf),
            pltpu.VMEM(held + (features,), bf),
            pltpu.VMEM(held + (features,), bf),
            pltpu.VMEM(held + (hidden,), bf),
            pltpu.VMEM(held + (hidden,), bf),
            pltpu.VMEM(held + (width,), fl),
            pltpu.VMEM((2,) + held + (hidden,), bf),
            pltpu.VMEM((2,) + held + (features,), bf),
            pltpu.VMEM(w_out.shape, bf),
            pltpu.VMEM((2, 2, SIDE, 16, HALF, width), bf),
            pltpu.VMEM((2, 2, 2, 16, HALF, width), bf),
            pltpu.VMEM((2, 2, 2, 16, HALF, width), bf),
            pltpu.VMEM((2, 2, SIDE, SIDE, HALF, features), bf),
            pltpu.VMEM((2, 2, 2, 2, HALF, features), bf),
            pltpu.VMEM((2, 2, 2, SIDE, HALF, features), bf),
            pltpu.VMEM((2, 2, SIDE, HALF, features), fl),
            pltpu.VMEM((2, 2, SIDE, HALF, features), bf),
            pltpu.VMEM((2, 2, 2, HALF, features // 2), bf),
            pltpu.VMEM((2, 2, 2, HALF, features), bf),
            pltpu.SemaphoreType.DMA((N_SEMS,)),
        ],
        compiler_params=pltpu.CompilerParams(
            collective_id=1, has_side_effects=True, vmem_limit_bytes=60 * 2**20
        ),
    )(x, dy, w_in, w_out)


def grads_kernel(x_ref, dh_ref, kept_ref, out_ref, grad_ref, w_in_grad, w_out_grad, out, grad):
    part = lax.dot_general(
        x_ref[...], dh_ref[...], (((0,), (0,)), ((), ())), preferred_element_type=jnp.float32
    )
    w_in_grad[...] = b16(part)
    w_out_grad[...] = kept_ref[...]

    @pl.when(pl.program_id(0) == 0)
    def _():
        out[...] = out_ref[...]
        grad[...] = grad_ref[...]


def per_device(layer_input, w_in, w_out, output_grad):
    out, grad, x_two, dh_two, kept = run_block(layer_input, output_grad, w_in, w_out)
    features, hidden = w_in.shape
    x_two, dh_two = x_two.reshape(-1, features), dh_two.reshape(-1, hidden)
    tokens, steps = x_two.shape[0], 4
    small = pl.BlockSpec(out.shape, lambda i: (0, 0))
    wide = pl.BlockSpec((features // steps, hidden), lambda i: (i, 0))
    tall = pl.BlockSpec((hidden // steps, features), lambda i: (i, 0))
    bf = jnp.bfloat16
    w_in_grad, w_out_grad, out, grad = pl.pallas_call(
        grads_kernel,
        grid=(steps,),
        out_shape=[jax.ShapeDtypeStruct(a.shape, bf) for a in (w_in, w_out, out, grad)],
        in_specs=[
            pl.BlockSpec((tokens, features // steps), lambda i: (0, i)),
            pl.BlockSpec((tokens, hidden), lambda i: (0, 0)),
            tall,
            small,
            small,
        ],
        out_specs=[wide, tall, small, small],
        compiler_params=pltpu.CompilerParams(vmem_limit_bytes=60 * 2**20),
    )(x_two, dh_two, kept, out, grad)
    return (out, grad, w_in_grad, w_out_grad)


def solution(mesh):
    in_specs = (
        P(("depth", "row"), "col"),
        P("col", "row"),
        P("row", "col"),
        P(("depth", "row"), "col"),
    )
    out_specs = (
        P(("depth", "row"), "col"),
        P(("depth", "row"), "col"),
        P("col", "row"),
        P("row", "col"),
    )
    return jax.shard_map(
        per_device, mesh=mesh, in_specs=in_specs, out_specs=out_specs, check_vma=False
    )
```

```python
import math

import jax
import jax.numpy as jnp
from jax import lax
from jax.experimental import pallas as pl
from jax.experimental.pallas import tpu as pltpu
from jax.sharding import PartitionSpec as P

MESH = pl.DeviceIdType.MESH
SIDE = 4
OWN, PREV, NEXT, FAR = range(4)
UNITS = (
    (
        ((OWN, 0, 3), (PREV, 0, 1), (NEXT, 0, 1)),
        ((PREV, 1, 3), (NEXT, 1, 3)),
        ((OWN, 3, 4), (PREV, 3, 4), (NEXT, 3, 4), (FAR, 0, 4)),
    ),
    (((OWN, 0, 4), (PREV, 0, 4), (NEXT, 0, 4), (FAR, 0, 4)),),
)
SIZES = tuple(tuple(sum(hi - lo for _, lo, hi in unit) for unit in units) for units in UNITS)
STARTS = tuple(tuple(sum(sizes[:unit]) for unit in range(len(sizes))) for sizes in SIZES)
HALF = 16
LO, HI = pl.ds(0, 2), pl.ds(2, 2)
BOTH = 2
GROUPS = {"others": (PREV, 3), "own": (OWN, 1)}
N_SEMS = 560


def gelu_parts(hidden):
    coeff = math.sqrt(2.0 / math.pi)
    square = hidden * hidden
    tangent = jnp.tanh(coeff * (hidden + 0.044715 * (square * hidden)))
    value = 0.5 * hidden * (1.0 + tangent)
    slope = 0.5 * (1.0 + tangent) + 0.5 * hidden * (1.0 - tangent * tangent) * coeff * (
        1.0 + 3.0 * 0.044715 * square
    )
    return (value, slope)


def f32(value):
    return value.astype(jnp.float32)


def b16(value):
    return value.astype(jnp.bfloat16)


class Ring:
    def __init__(self, after, before):
        self.after = after
        self.before = before


def block_kernel(
    x_ref, dy_ref, w_in_hbm, w_out_hbm,
    out_ref, grad_ref, x_hbm, dh_hbm, w_out_grad_hbm,
    w_in, w_out, x_all, dy_all, g_all, dh_all, slope, g_two, dy_two, w_out_grad,
    ysum, yfwd, yback, zsum, zfwd, zback, zown, xsum, xfwd, xback,
    sems,
):
    layer = lax.axis_index("depth")
    row = lax.axis_index("row")
    col = lax.axis_index("col")
    across, along = row // SIDE, row % SIDE

    def device(d, i, k, c):
        return (d, ((i + SIDE) % SIDE) * SIDE + (k + SIDE) % SIDE, (c + SIDE) % SIDE)

    ring_x = Ring(device(layer, across + 1, along, col), device(layer, across - 1, along, col))
    ring_z = Ring(device(layer, across, along + 1, col), device(layer, across, along - 1, col))
    ring_y = Ring(device(layer, across, along, col + 1), device(layer, across, along, col - 1))
    twin = (1 - layer, row, col)

    count = [0]
    sent = []

    def sem():
        count[0] += 1
        return sems.at[count[0] - 1]

    def send(src, dst, to):
        copy = pltpu.make_async_remote_copy(
            src_ref=src, dst_ref=dst, send_sem=sem(), recv_sem=sem(),
            device_id=to, device_id_type=MESH,
        )
        copy.start()
        sent.append(copy.wait_send)
        return copy

    def local(src, dst):
        copy = pltpu.make_async_copy(src, dst, sem())
        copy.start()
        return copy

    load_in = local(w_in_hbm, w_in)
    load_out = local(w_out_hbm, w_out)

    barrier = pltpu.get_barrier_semaphore()
    greeted = (ring_x.after, ring_x.before, ring_z.after, ring_z.before)
    greeted += (ring_y.after, ring_y.before, twin)
    for other in greeted:
        pl.semaphore_signal(barrier, inc=1, device_id=other, device_id_type=MESH)
    for half in range(2):
        rows = pl.ds(half * HALF, HALF)
        x_all[half, OWN, OWN] = x_ref[rows]
        dy_all[half, OWN, OWN] = dy_ref[rows]
    pl.semaphore_wait(barrier, len(greeted))

    kinds = ((x_all, ring_x, ring_z), (dy_all, ring_z, ring_x))
    features = x_all.shape[-1]
    left, right = pl.ds(0, features // 2), pl.ds(features // 2, features // 2)
    lines = {}
    planes = {}

    def share_block(kind, half, block):
        every, _, ring = kinds[kind]
        own = every.at[half, OWN, block]
        planes[kind, half, PREV, block] = send(own, every.at[half, PREV, block], ring.after)
        planes[kind, half, NEXT, block] = send(own, every.at[half, NEXT, block], ring.before)

    def open_line(kind, half):
        every, ring, _ = kinds[kind]
        own = every.at[half, OWN, OWN]
        lines[kind, half, PREV] = send(own, every.at[half, OWN, PREV], ring.after)
        lines[kind, half, NEXT] = send(own, every.at[half, OWN, NEXT], ring.before)

    def take_line(kind, half):
        every, ring, _ = kinds[kind]
        line = every.at[half, OWN]
        lines[kind, half, PREV].wait_recv()
        first = send(line.at[PREV, :, left], line.at[FAR, :, left], ring.after)
        lines[kind, half, NEXT].wait_recv()
        second = send(line.at[NEXT, :, right], line.at[FAR, :, right], ring.before)
        lines[kind, half, FAR] = (first, second)
        share_block(kind, half, PREV)
        share_block(kind, half, NEXT)

    def take_line_far(kind, half):
        for copy in lines[kind, half, FAR]:
            copy.wait_recv()
        share_block(kind, half, FAR)

    def take_block(kind, half, block):
        every, _, ring = kinds[kind]
        mine = every.at[half]
        planes[kind, half, PREV, block].wait_recv()
        if block in (OWN, PREV):
            copy = send(mine.at[PREV, block], mine.at[FAR, block], ring.after)
        planes[kind, half, NEXT, block].wait_recv()
        if block in (NEXT, FAR):
            copy = send(mine.at[NEXT, block], mine.at[FAR, block], ring.before)
        planes[kind, half, FAR, block] = copy

    def take_far(kind, half):
        for block in range(SIDE):
            planes[kind, half, FAR, block].wait_recv()

    for kind in range(2):
        open_line(kind, 0)
    for kind in range(2):
        share_block(kind, 0, OWN)

    width = slope.shape[-1]

    def rows_of(every, half, unit):
        parts = [every[half, plane, pl.ds(lo, hi - lo)] for plane, lo, hi in UNITS[half][unit]]
        part = parts[0] if len(parts) == 1 else jnp.concatenate(parts, axis=0)
        return part.reshape(part.shape[0] * part.shape[1], part.shape[2])

    def y_buffers(kind, half, unit):
        span = pl.ds(STARTS[half][unit], SIZES[half][unit])
        size = SIZES[half][unit]
        low, high = pl.ds(0, (size + 1) // 2), pl.ds((size + 1) // 2, size // 2)
        mine, fwd, back = ysum.at[kind, half, :, span], yfwd.at[kind, half], yback.at[kind, half]
        return mine, fwd.at[:, span], back.at[:, span], low, high

    sums = {}

    def y_product(kind, half, unit):
        mine, fwd, back, low, high = y_buffers(kind, half, unit)
        every = (x_all, dy_all)[kind]

        @pl.loop(0, 2, unroll=True)
        def _(tile):
            span = pl.ds(pl.multiple_of(tile * 2 * width, 2 * width), 2 * width)
            lhs = rows_of(every, half, unit)
            if kind == 0:
                part = jnp.dot(lhs, w_in[:, span], preferred_element_type=jnp.float32)
            else:
                part = lax.dot_general(
                    lhs, w_out[span, :], (((1,), (1,)), ((), ())),
                    preferred_element_type=jnp.float32,
                )
            part = b16(part)
            for piece in range(2):
                shard = (2 * tile + piece + SIDE - col) % SIDE
                cut = part[:, piece * width : (piece + 1) * width]
                mine[shard] = cut.reshape(SIZES[half][unit], HALF, width)

        sums[kind, half, unit] = [
            send(mine.at[2, high], fwd.at[0, high], ring_y.after),
            send(mine.at[2, low], fwd.at[1, low], ring_y.before),
            send(mine.at[1, low], back.at[0, low], ring_y.after),
            send(mine.at[3, high], back.at[1, high], ring_y.before),
        ]

    def y_relay(kind, half, unit):
        mine, fwd, back, low, high = y_buffers(kind, half, unit)
        copies = sums[kind, half, unit]
        copies[0].wait_recv()
        mine[1, high] = b16(f32(mine[1, high]) + f32(fwd[0, high]))
        copies.append(send(mine.at[1, high], back.at[0, high], ring_y.after))
        copies[1].wait_recv()
        mine[3, low] = b16(f32(mine[3, low]) + f32(fwd[1, low]))
        copies.append(send(mine.at[3, low], back.at[1, low], ring_y.before))

    def y_total(kind, half, unit):
        for copy in sums[kind, half, unit][2:]:
            copy.wait_recv()
        mine, _, back, _, _ = y_buffers(kind, half, unit)
        return f32(mine[0]) + f32(back[0]) + f32(back[1])

    own_columns = pl.ds(pl.multiple_of(col * width, width), width)

    def finish_hidden(half, unit):
        value, steep = gelu_parts(y_total(0, half, unit))
        value = b16(value)
        at = 0
        for plane, lo, hi in UNITS[half][unit]:
            span = pl.ds(lo, hi - lo)
            g_all[half, plane, span, :, own_columns] = value[at : at + hi - lo]
            slope[half, plane, span] = steep[at : at + hi - lo]
            at += hi - lo

    def finish_grad(half):
        for unit, pieces in enumerate(UNITS[half]):
            total = y_total(1, half, unit)
            at = 0
            for plane, lo, hi in pieces:
                for block in range(lo, hi):
                    part = b16(total[at] * slope[half, block, plane])
                    dh_all[half, plane, block, :, own_columns] = part
                    at += 1

    keep = []
    shared = []

    def share(src, dst):
        keep.append(local(src, dst))
        shared.append(send(src, dst, twin))

    def share_inputs(half):
        share(x_all.at[half], x_hbm.at[layer, half])
        for plane in range(SIDE):
            share(dy_all.at[half, plane], dy_two.at[layer, half, :, plane])

    def group_of(kind, half, group):
        first, size = GROUPS[group]
        every = (g_all, dh_all)[kind]
        if half == BOTH:
            return every.at[:, first]
        return every.at[half, pl.ds(first, size)]

    def columns_of(step):
        at = (col + step + SIDE) % SIDE
        return pl.ds(pl.multiple_of(at * width, width), width)

    passes = {}

    def start(kind, half, group):
        own = group_of(kind, half, group).at[:, :, :, own_columns]
        passes[kind, half, group] = [send(own, own, ring_y.after), send(own, own, ring_y.before)]

    def relay(kind, half, group):
        copies, every = passes[kind, half, group], group_of(kind, half, group)
        copies[0].wait_recv()
        part = every.at[:, LO, :, columns_of(-1)]
        copies.append(send(part, part, ring_y.after))
        copies[1].wait_recv()
        part = every.at[:, HI, :, columns_of(1)]
        copies.append(send(part, part, ring_y.before))

    def product(kind, half, group):
        first, size = GROUPS[group]
        every = (g_all, dh_all)[kind]

        @pl.loop(0, 4, unroll=True)
        def _(tile):
            cols = w_out.shape[1] // 4
            span = pl.ds(pl.multiple_of(tile * cols, cols), cols)
            lhs = every[:, first] if half == BOTH else every[half, pl.ds(first, size)]
            lhs = lhs.reshape(-1, every.shape[-1])
            if kind == 0:
                part = jnp.dot(lhs, w_out[:, span], preferred_element_type=jnp.float32)
            else:
                part = lax.dot_general(
                    lhs, w_in[span, :], (((1,), (1,)), ((), ())),
                    preferred_element_type=jnp.float32,
                )
            part = part.reshape(-1, SIDE, HALF, cols)
            if half == BOTH:
                zown[kind, :, :, :, span] = part
            elif first == OWN:
                zown[kind, half, :, :, span] = part[0]
            else:
                zsum[kind, half, pl.ds(first, size), :, :, span] = b16(part)

    moves = {}
    plane_rings = (ring_z, ring_x)
    block_rings = (ring_x, ring_z)

    def planes_start(kind, half):
        ring = plane_rings[kind]
        mine, fwd, back = zsum.at[kind, half], zfwd.at[kind, half], zback.at[kind, half]
        moves[kind, half, FAR] = (
            send(mine.at[FAR, HI], fwd.at[0], ring.after),
            send(mine.at[FAR, LO], fwd.at[1], ring.before),
        )
        moves[kind, half, OWN] = [
            send(mine.at[NEXT, LO], back.at[0, LO], ring.after),
            send(mine.at[PREV, HI], back.at[1, HI], ring.before),
        ]

    def planes_relay(kind, half):
        ring = plane_rings[kind]
        mine, fwd, back = zsum.at[kind, half], zfwd.at[kind, half], zback.at[kind, half]
        moves[kind, half, FAR][0].wait_recv()
        mine[NEXT, HI] = b16(f32(mine[NEXT, HI]) + f32(fwd[0]))
        moves[kind, half, OWN].append(send(mine.at[NEXT, HI], back.at[0, HI], ring.after))
        moves[kind, half, FAR][1].wait_recv()
        mine[PREV, LO] = b16(f32(mine[PREV, LO]) + f32(fwd[1]))
        moves[kind, half, OWN].append(send(mine.at[PREV, LO], back.at[1, LO], ring.before))

    lasts = {}

    def blocks_start(kind, half):
        ring = block_rings[kind]
        for copy in moves[kind, half, OWN]:
            copy.wait_recv()
        own, others = zown.at[kind, half], zback.at[kind, half]
        mine, fwd, back = xsum.at[kind, half], xfwd.at[kind, half], xback.at[kind, half]
        for block in (FAR, NEXT, PREV, OWN):
            total = own[block] + f32(others[0, block]) + f32(others[1, block])
            if block == OWN:
                own[OWN] = total
            else:
                mine[block] = b16(total)
        lasts[kind, half] = [
            send(mine.at[FAR, :, right], fwd.at[0], ring.after),
            send(mine.at[FAR, :, left], fwd.at[1], ring.before),
            send(mine.at[NEXT, :, left], back.at[0, :, left], ring.after),
            send(mine.at[PREV, :, right], back.at[1, :, right], ring.before),
        ]

    def blocks_relay(kind, half):
        ring, copies = block_rings[kind], lasts[kind, half]
        mine, fwd, back = xsum.at[kind, half], xfwd.at[kind, half], xback.at[kind, half]
        copies[0].wait_recv()
        mine[NEXT, :, right] = b16(f32(mine[NEXT, :, right]) + f32(fwd[0]))
        copies.append(send(mine.at[NEXT, :, right], back.at[0, :, right], ring.after))
        copies[1].wait_recv()
        mine[PREV, :, left] = b16(f32(mine[PREV, :, left]) + f32(fwd[1]))
        copies.append(send(mine.at[PREV, :, left], back.at[1, :, left], ring.before))

    def blocks_total(kind, half):
        for copy in lasts[kind, half][2:]:
            copy.wait_recv()
        rows = pl.ds(half * HALF, HALF)
        own, back = zown.at[kind, half], xback.at[kind, half]
        total = f32((x_ref, dy_ref)[kind][rows]) + own[OWN] + f32(back[0]) + f32(back[1])
        (out_ref, grad_ref)[kind][rows] = b16(total)

    def finish(kind, half, group):
        for copy in passes[kind, half, group][2:]:
            copy.wait_recv()
        first, size = GROUPS[group]
        for each in range(2) if half == BOTH else (half,):
            if kind == 0:
                span = pl.ds(first, size)
                share(g_all.at[each, span], g_two.at[layer, each, span])
            else:
                for plane in range(first, first + size):
                    share(dh_all.at[each, plane], dh_hbm.at[layer, each, :, plane])
        product(kind, half, group)
        if first != OWN:
            planes_start(kind, half)

    def settle():
        for copy in keep:
            copy.wait()
        for copy in shared:
            copy.wait_recv()
        keep.clear()
        shared.clear()

    def out_gradient(tile):
        rows = 512
        span = pl.ds(tile * rows, rows)

        @pl.loop(0, 2)
        def _(side):
            cols = dy_two.shape[-1] // 2
            part = pl.ds(pl.multiple_of(side * cols, cols), cols)
            lhs = g_two[:, :, :, :, :, span].reshape(-1, rows)
            rhs = dy_two[:, :, :, :, :, part].reshape(-1, cols)
            total = lax.dot_general(
                lhs, rhs, (((0,), (0,)), ((), ())), preferred_element_type=jnp.float32
            )
            w_out_grad[span, part] = b16(total)

        keep.append(local(w_out_grad.at[span], w_out_grad_hbm.at[span]))

    take_line(0, 0)
    take_line_far(0, 0)
    load_in.wait()
    open_line(0, 1)
    take_line(1, 0)
    load_out.wait()
    take_block(1, 0, OWN)
    y_product(1, 0, 0)
    take_block(0, 0, PREV)
    take_block(0, 0, OWN)
    take_block(0, 0, NEXT)
    y_product(0, 0, 0)
    take_block(0, 0, FAR)
    take_line_far(1, 0)
    y_product(0, 0, 1)
    take_line(0, 1)
    y_relay(1, 0, 0)
    y_relay(0, 0, 0)
    take_block(1, 0, NEXT)
    take_far(0, 0)
    y_product(0, 0, 2)
    take_block(1, 0, PREV)
    take_block(1, 0, FAR)
    share_block(0, 1, OWN)
    open_line(1, 1)
    y_product(1, 0, 1)
    take_line_far(0, 1)
    y_relay(0, 0, 1)
    share_block(1, 1, OWN)
    y_relay(0, 0, 2)
    take_far(1, 0)
    y_product(1, 0, 2)
    take_line(1, 1)
    take_block(0, 1, PREV)
    finish_hidden(0, 1)
    take_block(0, 1, FAR)
    y_relay(1, 0, 1)
    finish_hidden(0, 0)
    finish_hidden(0, 2)
    start(0, 0, "own")
    take_block(0, 1, NEXT)
    take_block(0, 1, OWN)
    start(0, 0, "others")
    take_block(1, 1, PREV)
    take_far(0, 1)
    take_line_far(1, 1)
    y_relay(1, 0, 2)
    relay(0, 0, "own")
    y_product(0, 1, 0)
    take_block(1, 1, NEXT)
    take_block(1, 1, OWN)
    share_inputs(0)
    relay(0, 0, "others")
    finish_grad(0)
    start(1, 0, "others")
    take_block(1, 1, FAR)
    take_far(1, 1)
    y_product(1, 1, 0)
    y_relay(0, 1, 0)
    finish(0, 0, "others")
    relay(1, 0, "others")
    y_relay(1, 1, 0)
    finish_hidden(1, 0)
    start(0, 1, "others")
    finish(1, 0, "others")
    start(0, 1, "own")
    finish_grad(1)
    start(1, 1, "others")
    planes_relay(0, 0)
    finish(0, 0, "own")
    relay(0, 1, "others")
    share_inputs(1)
    blocks_start(0, 0)
    planes_relay(1, 0)
    start(1, 0, "own")
    relay(1, 1, "others")
    finish(0, 1, "others")
    relay(0, 1, "own")
    relay(1, 0, "own")
    start(1, 1, "own")
    blocks_relay(0, 0)
    finish(1, 1, "others")
    finish(1, 0, "own")
    blocks_start(1, 0)
    relay(1, 1, "own")
    finish(0, 1, "own")
    planes_relay(0, 1)
    settle()
    planes_relay(1, 1)
    blocks_total(0, 0)
    out_gradient(0)
    finish(1, 1, "own")
    blocks_relay(1, 0)
    blocks_start(0, 1)
    blocks_start(1, 1)
    out_gradient(1)
    blocks_relay(0, 1)
    blocks_relay(1, 1)
    out_gradient(2)
    blocks_total(1, 0)
    blocks_total(0, 1)
    blocks_total(1, 1)

    for copy in keep:
        copy.wait()
    for copy in shared:
        copy.wait_recv()
    for wait_send in sent:
        wait_send()


def run_block(x, dy, w_in, w_out):
    tokens, features = x.shape
    hidden = w_in.shape[1]
    width = hidden // SIDE
    held = (2, SIDE, SIDE, HALF)
    bf, fl = jnp.bfloat16, jnp.float32
    vmem = pl.BlockSpec(memory_space=pltpu.VMEM)
    hbm = pl.BlockSpec(memory_space=pl.ANY)
    shape = jax.ShapeDtypeStruct
    return pl.pallas_call(
        block_kernel,
        out_shape=(
            shape((tokens, features), bf),
            shape((tokens, features), bf),
            shape((2,) + held + (features,), bf),
            shape((2,) + held + (hidden,), bf),
            shape(w_out.shape, bf),
        ),
        in_specs=[vmem, vmem, hbm, hbm],
        out_specs=(vmem, vmem, hbm, hbm, hbm),
        scratch_shapes=[
            pltpu.VMEM(w_in.shape, bf),
            pltpu.VMEM(w_out.shape, bf),
            pltpu.VMEM(held + (features,), bf),
            pltpu.VMEM(held + (features,), bf),
            pltpu.VMEM(held + (hidden,), bf),
            pltpu.VMEM(held + (hidden,), bf),
            pltpu.VMEM(held + (width,), fl),
            pltpu.VMEM((2,) + held + (hidden,), bf),
            pltpu.VMEM((2,) + held + (features,), bf),
            pltpu.VMEM(w_out.shape, bf),
            pltpu.VMEM((2, 2, SIDE, 16, HALF, width), bf),
            pltpu.VMEM((2, 2, 2, 16, HALF, width), bf),
            pltpu.VMEM((2, 2, 2, 16, HALF, width), bf),
            pltpu.VMEM((2, 2, SIDE, SIDE, HALF, features), bf),
            pltpu.VMEM((2, 2, 2, 2, HALF, features), bf),
            pltpu.VMEM((2, 2, 2, SIDE, HALF, features), bf),
            pltpu.VMEM((2, 2, SIDE, HALF, features), fl),
            pltpu.VMEM((2, 2, SIDE, HALF, features), bf),
            pltpu.VMEM((2, 2, 2, HALF, features // 2), bf),
            pltpu.VMEM((2, 2, 2, HALF, features), bf),
            pltpu.SemaphoreType.DMA((N_SEMS,)),
        ],
        compiler_params=pltpu.CompilerParams(
            collective_id=1, has_side_effects=True, vmem_limit_bytes=60 * 2**20
        ),
    )(x, dy, w_in, w_out)


def grads_kernel(x_ref, dh_ref, kept_ref, out_ref, grad_ref, w_in_grad, w_out_grad, out, grad):
    part = lax.dot_general(
        x_ref[...], dh_ref[...], (((0,), (0,)), ((), ())), preferred_element_type=jnp.float32
    )
    w_in_grad[...] = b16(part)
    w_out_grad[...] = kept_ref[...]

    @pl.when(pl.program_id(0) == 0)
    def _():
        out[...] = out_ref[...]
        grad[...] = grad_ref[...]


def per_device(layer_input, w_in, w_out, output_grad):
    out, grad, x_two, dh_two, kept = run_block(layer_input, output_grad, w_in, w_out)
    features, hidden = w_in.shape
    x_two, dh_two = x_two.reshape(-1, features), dh_two.reshape(-1, hidden)
    tokens, steps = x_two.shape[0], 4
    small = pl.BlockSpec(out.shape, lambda i: (0, 0))
    wide = pl.BlockSpec((features // steps, hidden), lambda i: (i, 0))
    tall = pl.BlockSpec((hidden // steps, features), lambda i: (i, 0))
    bf = jnp.bfloat16
    w_in_grad, w_out_grad, out, grad = pl.pallas_call(
        grads_kernel,
        grid=(steps,),
        out_shape=[jax.ShapeDtypeStruct(a.shape, bf) for a in (w_in, w_out, out, grad)],
        in_specs=[
            pl.BlockSpec((tokens, features // steps), lambda i: (0, i)),
            pl.BlockSpec((tokens, hidden), lambda i: (0, 0)),
            tall,
            small,
            small,
        ],
        out_specs=[wide, tall, small, small],
        compiler_params=pltpu.CompilerParams(vmem_limit_bytes=60 * 2**20),
    )(x_two, dh_two, kept, out, grad)
    return (out, grad, w_in_grad, w_out_grad)


def solution(mesh):
    in_specs = (
        P(("depth", "row"), "col"),
        P("col", "row"),
        P("row", "col"),
        P(("depth", "row"), "col"),
    )
    out_specs = (
        P(("depth", "row"), "col"),
        P(("depth", "row"), "col"),
        P("col", "row"),
        P("row", "col"),
    )
    return jax.shard_map(
        per_device, mesh=mesh, in_specs=in_specs, out_specs=out_specs, check_vma=False
    )
```

```python
import math

import jax
import jax.numpy as jnp
from jax import lax
from jax.experimental import pallas as pl
from jax.experimental.pallas import tpu as pltpu
from jax.sharding import PartitionSpec as P

MESH = pl.DeviceIdType.MESH
SIDE = 4
OWN, PREV, NEXT, FAR = range(4)
UNITS = (
    (
        ((OWN, 0, 3), (PREV, 0, 1), (NEXT, 0, 1)),
        ((PREV, 1, 3), (NEXT, 1, 3)),
        ((OWN, 3, 4), (PREV, 3, 4), (NEXT, 3, 4), (FAR, 0, 4)),
    ),
    (((OWN, 0, 4), (PREV, 0, 4), (NEXT, 0, 4), (FAR, 0, 4)),),
)
SIZES = tuple(tuple(sum(hi - lo for _, lo, hi in unit) for unit in units) for units in UNITS)
STARTS = tuple(tuple(sum(sizes[:unit]) for unit in range(len(sizes))) for sizes in SIZES)
HALF = 16
LO, HI = pl.ds(0, 2), pl.ds(2, 2)
BOTH = 2
GROUPS = {"others": (PREV, 3), "own": (OWN, 1)}
N_SEMS = 560


def gelu_parts(hidden):
    coeff = math.sqrt(2.0 / math.pi)
    square = hidden * hidden
    tangent = jnp.tanh(coeff * (hidden + 0.044715 * (square * hidden)))
    value = 0.5 * hidden * (1.0 + tangent)
    slope = 0.5 * (1.0 + tangent) + 0.5 * hidden * (1.0 - tangent * tangent) * coeff * (
        1.0 + 3.0 * 0.044715 * square
    )
    return (value, slope)


def f32(value):
    return value.astype(jnp.float32)


def b16(value):
    return value.astype(jnp.bfloat16)


class Ring:
    def __init__(self, after, before):
        self.after = after
        self.before = before


def block_kernel(
    x_hbm_in, dy_hbm_in, w_in_hbm, w_out_hbm,
    out_ref, grad_ref, x_hbm, dh_hbm, w_out_grad_hbm,
    w_in, w_out, x_all, dy_all, g_all, dh_all, slope, g_two, dy_two, w_out_grad,
    ysum, yfwd, yback, zsum, zfwd, zback, zown, xsum, xfwd, xback,
    sems,
):
    layer = lax.axis_index("depth")
    row = lax.axis_index("row")
    col = lax.axis_index("col")
    across, along = row // SIDE, row % SIDE

    def device(d, i, k, c):
        return (d, ((i + SIDE) % SIDE) * SIDE + (k + SIDE) % SIDE, (c + SIDE) % SIDE)

    ring_x = Ring(device(layer, across + 1, along, col), device(layer, across - 1, along, col))
    ring_z = Ring(device(layer, across, along + 1, col), device(layer, across, along - 1, col))
    ring_y = Ring(device(layer, across, along, col + 1), device(layer, across, along, col - 1))
    twin = (1 - layer, row, col)

    count = [0]
    sent = []

    def sem():
        count[0] += 1
        return sems.at[count[0] - 1]

    def send(src, dst, to):
        copy = pltpu.make_async_remote_copy(
            src_ref=src, dst_ref=dst, send_sem=sem(), recv_sem=sem(),
            device_id=to, device_id_type=MESH,
        )
        copy.start()
        sent.append(copy.wait_send)
        return copy

    def local(src, dst):
        copy = pltpu.make_async_copy(src, dst, sem())
        copy.start()
        return copy

    own = []
    for half in range(2):
        rows = pl.ds(half * HALF, HALF)
        own.append(local(x_hbm_in.at[rows], x_all.at[half, OWN, OWN]))
        own.append(local(dy_hbm_in.at[rows], dy_all.at[half, OWN, OWN]))
    load_in = local(w_in_hbm, w_in)
    load_out = local(w_out_hbm, w_out)

    barrier = pltpu.get_barrier_semaphore()
    greeted = (ring_x.after, ring_x.before, ring_z.after, ring_z.before)
    greeted += (ring_y.after, ring_y.before, twin)
    for other in greeted:
        pl.semaphore_signal(barrier, inc=1, device_id=other, device_id_type=MESH)
    for copy in own:
        copy.wait()
    pl.semaphore_wait(barrier, len(greeted))

    kinds = ((x_all, ring_x, ring_z), (dy_all, ring_z, ring_x))
    features = x_all.shape[-1]
    left, right = pl.ds(0, features // 2), pl.ds(features // 2, features // 2)
    lines = {}
    planes = {}

    def share_block(kind, half, block):
        every, _, ring = kinds[kind]
        own = every.at[half, OWN, block]
        planes[kind, half, PREV, block] = send(own, every.at[half, PREV, block], ring.after)
        planes[kind, half, NEXT, block] = send(own, every.at[half, NEXT, block], ring.before)

    def open_line(kind, half):
        every, ring, _ = kinds[kind]
        own = every.at[half, OWN, OWN]
        lines[kind, half, PREV] = send(own, every.at[half, OWN, PREV], ring.after)
        lines[kind, half, NEXT] = send(own, every.at[half, OWN, NEXT], ring.before)

    def take_line(kind, half):
        every, ring, _ = kinds[kind]
        line = every.at[half, OWN]
        lines[kind, half, PREV].wait_recv()
        first = send(line.at[PREV, :, left], line.at[FAR, :, left], ring.after)
        lines[kind, half, NEXT].wait_recv()
        second = send(line.at[NEXT, :, right], line.at[FAR, :, right], ring.before)
        lines[kind, half, FAR] = (first, second)
        share_block(kind, half, PREV)
        share_block(kind, half, NEXT)

    def take_line_far(kind, half):
        for copy in lines[kind, half, FAR]:
            copy.wait_recv()
        share_block(kind, half, FAR)

    def take_block(kind, half, block):
        every, _, ring = kinds[kind]
        mine = every.at[half]
        planes[kind, half, PREV, block].wait_recv()
        if block in (OWN, PREV):
            copy = send(mine.at[PREV, block], mine.at[FAR, block], ring.after)
        planes[kind, half, NEXT, block].wait_recv()
        if block in (NEXT, FAR):
            copy = send(mine.at[NEXT, block], mine.at[FAR, block], ring.before)
        planes[kind, half, FAR, block] = copy

    def take_far(kind, half):
        for block in range(SIDE):
            planes[kind, half, FAR, block].wait_recv()

    for kind in range(2):
        open_line(kind, 0)
    for kind in range(2):
        share_block(kind, 0, OWN)

    width = slope.shape[-1]

    def rows_of(every, half, unit):
        parts = [every[half, plane, pl.ds(lo, hi - lo)] for plane, lo, hi in UNITS[half][unit]]
        part = parts[0] if len(parts) == 1 else jnp.concatenate(parts, axis=0)
        return part.reshape(part.shape[0] * part.shape[1], part.shape[2])

    def y_buffers(kind, half, unit):
        span = pl.ds(STARTS[half][unit], SIZES[half][unit])
        size = SIZES[half][unit]
        low, high = pl.ds(0, (size + 1) // 2), pl.ds((size + 1) // 2, size // 2)
        mine, fwd, back = ysum.at[kind, half, :, span], yfwd.at[kind, half], yback.at[kind, half]
        return mine, fwd.at[:, span], back.at[:, span], low, high

    sums = {}

    def y_product(kind, half, unit):
        mine, fwd, back, low, high = y_buffers(kind, half, unit)
        every = (x_all, dy_all)[kind]

        @pl.loop(0, 2, unroll=True)
        def _(tile):
            span = pl.ds(pl.multiple_of(tile * 2 * width, 2 * width), 2 * width)
            lhs = rows_of(every, half, unit)
            if kind == 0:
                part = jnp.dot(lhs, w_in[:, span], preferred_element_type=jnp.float32)
            else:
                part = lax.dot_general(
                    lhs, w_out[span, :], (((1,), (1,)), ((), ())),
                    preferred_element_type=jnp.float32,
                )
            part = b16(part)
            for piece in range(2):
                shard = (2 * tile + piece + SIDE - col) % SIDE
                cut = part[:, piece * width : (piece + 1) * width]
                mine[shard] = cut.reshape(SIZES[half][unit], HALF, width)

        sums[kind, half, unit] = [
            send(mine.at[2, high], fwd.at[0, high], ring_y.after),
            send(mine.at[2, low], fwd.at[1, low], ring_y.before),
            send(mine.at[1, low], back.at[0, low], ring_y.after),
            send(mine.at[3, high], back.at[1, high], ring_y.before),
        ]

    def y_relay(kind, half, unit):
        mine, fwd, back, low, high = y_buffers(kind, half, unit)
        copies = sums[kind, half, unit]
        copies[0].wait_recv()
        mine[1, high] = b16(f32(mine[1, high]) + f32(fwd[0, high]))
        copies.append(send(mine.at[1, high], back.at[0, high], ring_y.after))
        copies[1].wait_recv()
        mine[3, low] = b16(f32(mine[3, low]) + f32(fwd[1, low]))
        copies.append(send(mine.at[3, low], back.at[1, low], ring_y.before))

    def y_total(kind, half, unit):
        for copy in sums[kind, half, unit][2:]:
            copy.wait_recv()
        mine, _, back, _, _ = y_buffers(kind, half, unit)
        return f32(mine[0]) + f32(back[0]) + f32(back[1])

    own_columns = pl.ds(pl.multiple_of(col * width, width), width)

    def finish_hidden(half, unit):
        value, steep = gelu_parts(y_total(0, half, unit))
        value = b16(value)
        at = 0
        for plane, lo, hi in UNITS[half][unit]:
            span = pl.ds(lo, hi - lo)
            g_all[half, plane, span, :, own_columns] = value[at : at + hi - lo]
            slope[half, plane, span] = steep[at : at + hi - lo]
            at += hi - lo

    def finish_grad(half):
        for unit, pieces in enumerate(UNITS[half]):
            total = y_total(1, half, unit)
            at = 0
            for plane, lo, hi in pieces:
                for block in range(lo, hi):
                    part = b16(total[at] * slope[half, block, plane])
                    dh_all[half, plane, block, :, own_columns] = part
                    at += 1

    keep = []
    shared = []

    def share(src, dst):
        keep.append(local(src, dst))
        shared.append(send(src, dst, twin))

    def share_inputs(half):
        share(x_all.at[half], x_hbm.at[layer, half])
        for plane in range(SIDE):
            share(dy_all.at[half, plane], dy_two.at[layer, half, :, plane])

    def group_of(kind, half, group):
        first, size = GROUPS[group]
        every = (g_all, dh_all)[kind]
        if half == BOTH:
            return every.at[:, first]
        return every.at[half, pl.ds(first, size)]

    def columns_of(step):
        at = (col + step + SIDE) % SIDE
        return pl.ds(pl.multiple_of(at * width, width), width)

    passes = {}

    def start(kind, half, group):
        own = group_of(kind, half, group).at[:, :, :, own_columns]
        passes[kind, half, group] = [send(own, own, ring_y.after), send(own, own, ring_y.before)]

    def relay(kind, half, group):
        copies, every = passes[kind, half, group], group_of(kind, half, group)
        copies[0].wait_recv()
        part = every.at[:, LO, :, columns_of(-1)]
        copies.append(send(part, part, ring_y.after))
        copies[1].wait_recv()
        part = every.at[:, HI, :, columns_of(1)]
        copies.append(send(part, part, ring_y.before))

    def product(kind, half, group):
        first, size = GROUPS[group]
        every = (g_all, dh_all)[kind]

        @pl.loop(0, 2, unroll=True)
        def _(tile):
            cols = w_out.shape[1] // 2
            span = pl.ds(pl.multiple_of(tile * cols, cols), cols)
            lhs = every[:, first] if half == BOTH else every[half, pl.ds(first, size)]
            lhs = lhs.reshape(-1, every.shape[-1])
            if kind == 0:
                part = jnp.dot(lhs, w_out[:, span], preferred_element_type=jnp.float32)
            else:
                part = lax.dot_general(
                    lhs, w_in[span, :], (((1,), (1,)), ((), ())),
                    preferred_element_type=jnp.float32,
                )
            part = part.reshape(-1, SIDE, HALF, cols)
            if half == BOTH:
                zown[kind, :, :, :, span] = part
            elif first == OWN:
                zown[kind, half, :, :, span] = part[0]
            else:
                zsum[kind, half, pl.ds(first, size), :, :, span] = b16(part)

    moves = {}
    plane_rings = (ring_z, ring_x)
    block_rings = (ring_x, ring_z)

    def planes_start(kind, half):
        ring = plane_rings[kind]
        mine, fwd, back = zsum.at[kind, half], zfwd.at[kind, half], zback.at[kind, half]
        moves[kind, half, FAR] = (
            send(mine.at[FAR, HI], fwd.at[0], ring.after),
            send(mine.at[FAR, LO], fwd.at[1], ring.before),
        )
        moves[kind, half, OWN] = [
            send(mine.at[NEXT, LO], back.at[0, LO], ring.after),
            send(mine.at[PREV, HI], back.at[1, HI], ring.before),
        ]

    def planes_relay(kind, half):
        ring = plane_rings[kind]
        mine, fwd, back = zsum.at[kind, half], zfwd.at[kind, half], zback.at[kind, half]
        moves[kind, half, FAR][0].wait_recv()
        mine[NEXT, HI] = b16(f32(mine[NEXT, HI]) + f32(fwd[0]))
        moves[kind, half, OWN].append(send(mine.at[NEXT, HI], back.at[0, HI], ring.after))
        moves[kind, half, FAR][1].wait_recv()
        mine[PREV, LO] = b16(f32(mine[PREV, LO]) + f32(fwd[1]))
        moves[kind, half, OWN].append(send(mine.at[PREV, LO], back.at[1, LO], ring.before))

    lasts = {}

    def blocks_start(kind, half):
        ring = block_rings[kind]
        for copy in moves[kind, half, OWN]:
            copy.wait_recv()
        own, others = zown.at[kind, half], zback.at[kind, half]
        mine, fwd, back = xsum.at[kind, half], xfwd.at[kind, half], xback.at[kind, half]
        for block in (FAR, NEXT, PREV, OWN):
            total = own[block] + f32(others[0, block]) + f32(others[1, block])
            if block == OWN:
                own[OWN] = total
            else:
                mine[block] = b16(total)
        lasts[kind, half] = [
            send(mine.at[FAR, :, right], fwd.at[0], ring.after),
            send(mine.at[FAR, :, left], fwd.at[1], ring.before),
            send(mine.at[NEXT, :, left], back.at[0, :, left], ring.after),
            send(mine.at[PREV, :, right], back.at[1, :, right], ring.before),
        ]

    def blocks_relay(kind, half):
        ring, copies = block_rings[kind], lasts[kind, half]
        mine, fwd, back = xsum.at[kind, half], xfwd.at[kind, half], xback.at[kind, half]
        copies[0].wait_recv()
        mine[NEXT, :, right] = b16(f32(mine[NEXT, :, right]) + f32(fwd[0]))
        copies.append(send(mine.at[NEXT, :, right], back.at[0, :, right], ring.after))
        copies[1].wait_recv()
        mine[PREV, :, left] = b16(f32(mine[PREV, :, left]) + f32(fwd[1]))
        copies.append(send(mine.at[PREV, :, left], back.at[1, :, left], ring.before))

    def blocks_total(kind, half):
        for copy in lasts[kind, half][2:]:
            copy.wait_recv()
        rows = pl.ds(half * HALF, HALF)
        own, back = zown.at[kind, half], xback.at[kind, half]
        total = f32((x_all, dy_all)[kind][half, OWN, OWN]) + own[OWN] + f32(back[0]) + f32(back[1])
        (out_ref, grad_ref)[kind][rows] = b16(total)

    def finish(kind, half, group):
        for copy in passes[kind, half, group][2:]:
            copy.wait_recv()
        first, size = GROUPS[group]
        for each in range(2) if half == BOTH else (half,):
            if kind == 0:
                span = pl.ds(first, size)
                share(g_all.at[each, span], g_two.at[layer, each, span])
            else:
                for plane in range(first, first + size):
                    share(dh_all.at[each, plane], dh_hbm.at[layer, each, :, plane])
        product(kind, half, group)
        if first != OWN:
            planes_start(kind, half)

    def settle():
        for copy in keep:
            copy.wait()
        for copy in shared:
            copy.wait_recv()
        keep.clear()
        shared.clear()

    def out_gradient(tile):
        rows = 512
        span = pl.ds(tile * rows, rows)

        @pl.loop(0, 2)
        def _(side):
            cols = dy_two.shape[-1] // 2
            part = pl.ds(pl.multiple_of(side * cols, cols), cols)
            lhs = g_two[:, :, :, :, :, span].reshape(-1, rows)
            rhs = dy_two[:, :, :, :, :, part].reshape(-1, cols)
            total = lax.dot_general(
                lhs, rhs, (((0,), (0,)), ((), ())), preferred_element_type=jnp.float32
            )
            w_out_grad[span, part] = b16(total)

        keep.append(local(w_out_grad.at[span], w_out_grad_hbm.at[span]))

    take_line(0, 0)
    take_line_far(0, 0)
    load_in.wait()
    open_line(0, 1)
    take_line(1, 0)
    load_out.wait()
    take_block(1, 0, OWN)
    y_product(1, 0, 0)
    take_block(0, 0, PREV)
    take_block(0, 0, OWN)
    take_block(0, 0, NEXT)
    y_product(0, 0, 0)
    take_block(0, 0, FAR)
    take_line_far(1, 0)
    y_product(0, 0, 1)
    take_line(0, 1)
    y_relay(1, 0, 0)
    y_relay(0, 0, 0)
    take_block(1, 0, NEXT)
    take_far(0, 0)
    y_product(0, 0, 2)
    take_block(1, 0, PREV)
    take_block(1, 0, FAR)
    share_block(0, 1, OWN)
    open_line(1, 1)
    y_product(1, 0, 1)
    take_line_far(0, 1)
    y_relay(0, 0, 1)
    share_block(1, 1, OWN)
    y_relay(0, 0, 2)
    take_far(1, 0)
    y_product(1, 0, 2)
    take_line(1, 1)
    take_block(0, 1, PREV)
    finish_hidden(0, 1)
    take_block(0, 1, FAR)
    y_relay(1, 0, 1)
    finish_hidden(0, 0)
    finish_hidden(0, 2)
    start(0, 0, "own")
    take_block(0, 1, NEXT)
    take_block(0, 1, OWN)
    start(0, 0, "others")
    take_block(1, 1, PREV)
    take_far(0, 1)
    take_line_far(1, 1)
    y_relay(1, 0, 2)
    relay(0, 0, "own")
    y_product(0, 1, 0)
    take_block(1, 1, NEXT)
    take_block(1, 1, OWN)
    share_inputs(0)
    relay(0, 0, "others")
    finish_grad(0)
    start(1, 0, "others")
    take_block(1, 1, FAR)
    take_far(1, 1)
    y_product(1, 1, 0)
    y_relay(0, 1, 0)
    finish(0, 0, "others")
    relay(1, 0, "others")
    y_relay(1, 1, 0)
    finish_hidden(1, 0)
    start(0, 1, "others")
    finish(1, 0, "others")
    start(0, 1, "own")
    finish_grad(1)
    start(1, 1, "others")
    planes_relay(0, 0)
    finish(0, 0, "own")
    relay(0, 1, "others")
    share_inputs(1)
    blocks_start(0, 0)
    planes_relay(1, 0)
    start(1, 0, "own")
    relay(1, 1, "others")
    finish(0, 1, "others")
    relay(0, 1, "own")
    relay(1, 0, "own")
    start(1, 1, "own")
    blocks_relay(0, 0)
    finish(1, 1, "others")
    finish(1, 0, "own")
    blocks_start(1, 0)
    relay(1, 1, "own")
    finish(0, 1, "own")
    planes_relay(0, 1)
    settle()
    planes_relay(1, 1)
    blocks_total(0, 0)
    out_gradient(0)
    finish(1, 1, "own")
    blocks_relay(1, 0)
    blocks_start(0, 1)
    blocks_start(1, 1)
    out_gradient(1)
    blocks_relay(0, 1)
    blocks_relay(1, 1)
    out_gradient(2)
    blocks_total(1, 0)
    blocks_total(0, 1)
    blocks_total(1, 1)

    for copy in keep:
        copy.wait()
    for copy in shared:
        copy.wait_recv()
    for wait_send in sent:
        wait_send()


def run_block(x, dy, w_in, w_out):
    tokens, features = x.shape
    hidden = w_in.shape[1]
    width = hidden // SIDE
    held = (2, SIDE, SIDE, HALF)
    bf, fl = jnp.bfloat16, jnp.float32
    vmem = pl.BlockSpec(memory_space=pltpu.VMEM)
    hbm = pl.BlockSpec(memory_space=pl.ANY)
    shape = jax.ShapeDtypeStruct
    return pl.pallas_call(
        block_kernel,
        out_shape=(
            shape((tokens, features), bf),
            shape((tokens, features), bf),
            shape((2,) + held + (features,), bf),
            shape((2,) + held + (hidden,), bf),
            shape(w_out.shape, bf),
        ),
        in_specs=[hbm, hbm, hbm, hbm],
        out_specs=(vmem, vmem, hbm, hbm, hbm),
        scratch_shapes=[
            pltpu.VMEM(w_in.shape, bf),
            pltpu.VMEM(w_out.shape, bf),
            pltpu.VMEM(held + (features,), bf),
            pltpu.VMEM(held + (features,), bf),
            pltpu.VMEM(held + (hidden,), bf),
            pltpu.VMEM(held + (hidden,), bf),
            pltpu.VMEM(held + (width,), fl),
            pltpu.VMEM((2,) + held + (hidden,), bf),
            pltpu.VMEM((2,) + held + (features,), bf),
            pltpu.VMEM(w_out.shape, bf),
            pltpu.VMEM((2, 2, SIDE, 16, HALF, width), bf),
            pltpu.VMEM((2, 2, 2, 16, HALF, width), bf),
            pltpu.VMEM((2, 2, 2, 16, HALF, width), bf),
            pltpu.VMEM((2, 2, SIDE, SIDE, HALF, features), bf),
            pltpu.VMEM((2, 2, 2, 2, HALF, features), bf),
            pltpu.VMEM((2, 2, 2, SIDE, HALF, features), bf),
            pltpu.VMEM((2, 2, SIDE, HALF, features), fl),
            pltpu.VMEM((2, 2, SIDE, HALF, features), bf),
            pltpu.VMEM((2, 2, 2, HALF, features // 2), bf),
            pltpu.VMEM((2, 2, 2, HALF, features), bf),
            pltpu.SemaphoreType.DMA((N_SEMS,)),
        ],
        compiler_params=pltpu.CompilerParams(
            collective_id=1, has_side_effects=True, vmem_limit_bytes=60 * 2**20
        ),
    )(x, dy, w_in, w_out)


def grads_kernel(x_ref, dh_ref, kept_ref, out_ref, grad_ref, w_in_grad, w_out_grad, out, grad):
    part = lax.dot_general(
        x_ref[...], dh_ref[...], (((0,), (0,)), ((), ())), preferred_element_type=jnp.float32
    )
    w_in_grad[...] = b16(part)
    w_out_grad[...] = kept_ref[...]

    @pl.when(pl.program_id(0) == 0)
    def _():
        out[...] = out_ref[...]
        grad[...] = grad_ref[...]


def per_device(layer_input, w_in, w_out, output_grad):
    out, grad, x_two, dh_two, kept = run_block(layer_input, output_grad, w_in, w_out)
    features, hidden = w_in.shape
    x_two, dh_two = x_two.reshape(-1, features), dh_two.reshape(-1, hidden)
    tokens, steps = x_two.shape[0], 4
    small = pl.BlockSpec(out.shape, lambda i: (0, 0))
    wide = pl.BlockSpec((features // steps, hidden), lambda i: (i, 0))
    tall = pl.BlockSpec((hidden // steps, features), lambda i: (i, 0))
    bf = jnp.bfloat16
    w_in_grad, w_out_grad, out, grad = pl.pallas_call(
        grads_kernel,
        grid=(steps,),
        out_shape=[jax.ShapeDtypeStruct(a.shape, bf) for a in (w_in, w_out, out, grad)],
        in_specs=[
            pl.BlockSpec((tokens, features // steps), lambda i: (0, i)),
            pl.BlockSpec((tokens, hidden), lambda i: (0, 0)),
            tall,
            small,
            small,
        ],
        out_specs=[wide, tall, small, small],
        compiler_params=pltpu.CompilerParams(vmem_limit_bytes=60 * 2**20),
    )(x_two, dh_two, kept, out, grad)
    return (out, grad, w_in_grad, w_out_grad)


def solution(mesh):
    in_specs = (
        P(("depth", "row"), "col"),
        P("col", "row"),
        P("row", "col"),
        P(("depth", "row"), "col"),
    )
    out_specs = (
        P(("depth", "row"), "col"),
        P(("depth", "row"), "col"),
        P("col", "row"),
        P("row", "col"),
    )
    return jax.shard_map(
        per_device, mesh=mesh, in_specs=in_specs, out_specs=out_specs, check_vma=False
    )
```
